32 devices in a mesh: dom: 16 (over z, y, x), sub: 2 (over core).
Axes of the slice: x: 2, y: 2, z: 4, core: 2. Of those that a mesh axis runs over, the one named last changes fastest.
Arguments:
- a_blocks: bfloat16 [2048, 8, 128, 128], P(('dom', 'sub')), may hold values from -6 to 6
- nbr_offset: int32 [2048, 8], P(('dom', 'sub')), may hold values from -3 to 3
- nbr_count: int32 [2048], P(('dom', 'sub')), may hold values from 4 to 8
- prolong: bfloat16 [2048, 128, 128], P(('dom', 'sub')), may hold values from -0.5 to 0.5
- owner_start: int32 [32], replicated, may hold values from 0 to 2047, as said below
Outputs:
- coarse: float32 [512, 7, 128, 128], P(('dom', 'sub'))
The draws below stay inside these ranges and needn't reach their ends.
Inputs may be any that keep to these rules, and one draw needn't show every extreme that they name: owner_start[0] = 0, owner_start[1] = 112, and owner_start[d] - d * 64 lies in 0 to 48 for every d.
All inputs are finite; a program needn't handle non-finite values.
Results may differ from the reference program's by a relative error of at most 0.0029.
Values may be sent and summed in bfloat16 or wider, within the bound.
No kernel may reach another device: no remote copies, remote signals or barrier semaphores. Data moves between devices by JAX's collectives and lax.ppermute only.
A program may use at most 256 MiB of HBM per device.

```python
import jax
import jax.numpy as jnp
from jax import lax

B = 128
BC = 128
K = 8
W = 3
KC = 7
RB = 64
AD = 16
EMAX = 48
NF = 2048
NA = 512


def draw_owner_start(key, part):
    count_owners = NF // RB
    shifts = jax.random.randint(key, (count_owners,), 0, EMAX + 1)
    owner_index = jnp.arange(count_owners, dtype=jnp.int32)
    shifts = jnp.where(owner_index == 0, 0, jnp.where(owner_index == 1, EMAX, shifts))
    return (owner_index * RB + shifts).astype(jnp.int32)


def with_ends(values, stream_key, smallest, high):
    shape = values.shape
    place = [jax.random.randint(jax.random.fold_in(stream_key, axis), (), 0, shape[axis]) for axis in range(len(shape))]
    values = values.at[tuple(place)].set(smallest)
    longest = shape.index(max(shape))
    place[longest] = (place[longest] + 1) % shape[longest]
    return values.at[tuple(place)].set(high)


def block_scale(stream_key, dims, pieces, smallest, top_value):
    def one(axis_at, shards_of):
        heights = jax.random.uniform(jax.random.fold_in(jax.random.fold_in(stream_key, 6), axis_at), (shards_of,), jnp.float32, smallest / len(pieces), top_value / len(pieces))
        return jnp.repeat(jnp.exp(heights), dims[axis_at] // shards_of).reshape((-1,) + (1,) * (len(dims) - axis_at - 1))

    loudness = one(*pieces[0])
    for cut in pieces[1:]:
        loudness = loudness * one(*cut)
    return loudness


def gaussian(rng, dims, scale, most, split=(), held_as=jnp.bfloat16):
    entries = jax.random.normal(rng, dims, jnp.float32) * scale
    if len(split) > 0:
        entries = block_scale(rng, dims, split, -0.22, 0.18) * entries
    return jnp.clip(entries, min=-most, max=most).astype(held_as)


def setup_inputs(seed: int = 0) -> dict:
    seeds = jax.random.split(jax.random.key(seed), 6)
    a_blocks = gaussian(seeds[0], (NF, K, B, B), 0.4, 6.0, ((0, 32),))
    nbr_offset = with_ends(jax.random.randint(seeds[1], (NF, K), 0 - W, W + 1), jax.random.fold_in(seeds[1], 1), 0 - W, W).astype(jnp.int32)
    nbr_count = with_ends(jax.random.randint(seeds[2], (NF,), K // 2, K + 1), jax.random.fold_in(seeds[2], 1), K // 2, K).astype(jnp.int32)
    prolong = gaussian(seeds[3], (NF, B, BC), B ** -0.5, 0.5, ((0, 32),))
    owner_start = draw_owner_start(jax.random.fold_in(seeds[5], 71), 0)
    return {"a_blocks": a_blocks, "nbr_offset": nbr_offset, "nbr_count": nbr_count, "prolong": prolong, "owner_start": owner_start}


def aggregate_ids(fine_ids, owner_start, total_rows):
    flat_ids = fine_ids.reshape(-1)
    bounds = jnp.concatenate([owner_start, jnp.full((1,), total_rows, jnp.int32)])
    owner_index = jnp.sum((owner_start[None, :] <= flat_ids[:, None]).astype(jnp.int32), axis=1) - 1
    first_row = bounds[owner_index]
    span_rows = bounds[owner_index + 1] - first_row
    local_ids = ((flat_ids - first_row) * AD) // span_rows
    return (owner_index * AD + local_ids).astype(jnp.int32).reshape(fine_ids.shape)


def galerkin_rows(blocks, window, offsets, counts, fine_ids, owner_start, total_rows):
    count_rows = blocks.shape[0]
    local_index = jnp.arange(count_rows, dtype=jnp.int32)[:, None] + W + offsets
    near_rows = window[local_index].astype(jnp.float32)
    products = jnp.einsum("rkab,rkbc->rkac", blocks.astype(jnp.float32), near_rows, precision=lax.Precision.HIGHEST)
    neighbour = fine_ids[:, None] + offsets
    is_valid = (jnp.arange(K, dtype=jnp.int32)[None, :] < counts[:, None]) & (neighbour >= 0) & (neighbour < total_rows)
    row_aggs = aggregate_ids(jnp.clip(fine_ids, 0, total_rows - 1), owner_start, total_rows)
    slot_index = aggregate_ids(jnp.clip(neighbour, 0, total_rows - 1), owner_start, total_rows) - row_aggs[:, None] + W
    select = ((slot_index[..., None] == jnp.arange(KC, dtype=jnp.int32)) & is_valid[..., None]).astype(jnp.float32)
    applied = jnp.einsum("rkq,rkac->rqac", select, products, precision=lax.Precision.HIGHEST).astype(jnp.bfloat16)
    own_rows = window[W:W + count_rows].astype(jnp.float32)
    return jnp.einsum("rbx,rqby->rqxy", own_rows, applied.astype(jnp.float32), precision=lax.Precision.HIGHEST)


def reference(a_blocks, nbr_offset, nbr_count, prolong, owner_start):
    padded = jnp.pad(prolong, ((W, W), (0, 0), (0, 0)))

    def add_group(group_index, coarse):
        first = (group_index * RB).astype(jnp.int32)
        blocks = lax.dynamic_slice_in_dim(a_blocks, first, RB, 0)
        offsets = lax.dynamic_slice_in_dim(nbr_offset, first, RB, 0)
        counts = lax.dynamic_slice_in_dim(nbr_count, first, RB, 0)
        window = lax.dynamic_slice_in_dim(padded, first, RB + 2 * W, 0)
        fine_ids = first + jnp.arange(RB, dtype=jnp.int32)
        terms = galerkin_rows(blocks, window, offsets, counts, fine_ids, owner_start, NF)
        row_aggs = aggregate_ids(fine_ids, owner_start, NF)
        return coarse.at[row_aggs].add(terms)

    start_value = jnp.zeros((NA, KC, BC, BC), jnp.float32)
    return lax.fori_loop(0, NF // RB, add_group, start_value)
```

```python
import functools

import jax
import jax.numpy as jnp
from jax import lax
from jax.experimental import pallas as pl
from jax.experimental.pallas import tpu as pltpu
from jax.sharding import PartitionSpec as P

W = 3
KC = 7
AD = 16
SMAX = 48
NQ = 4
UNROLL = 4
HALF = 22
AXES = ("dom", "sub")

T_AGG = 0
T_OFF = 128
T_BASE = 256
T_DST = 384
T_N = 448
T_H = 449
T_LO = 450
T_HI = 451
T_S = 452
T_LEN = 512


def scan_rows(pos, devices, rows, own_ref, table):
    def start(owner):
        inside = (owner >= 0) & (owner < devices)
        at = jnp.clip(owner, 0, devices - 1)
        return jnp.where(inside, own_ref[at], jnp.where(owner < 0, 0, devices * rows))

    total = devices * rows
    first = pos * rows
    begin0, begin1, begin2, begin3 = (start(pos - 1), start(pos), start(pos + 1), start(pos + 2))
    row = jnp.maximum(first - W, 0)
    below = row < begin1
    length = jnp.maximum(jnp.where(below, begin1 - begin0, begin2 - begin1), 1)
    scaled = (row - jnp.where(below, begin0, begin1)) * AD
    local = lax.div(scaled, length)
    agg = jnp.where(below, 0, AD) + local
    rest = scaled - local * length

    def step(at, carry):
        agg, rest = carry
        table[T_AGG + at] = agg
        here = first + at - W
        moves = (here >= 0) & (here < total - 1)
        then = here + 1
        length = jnp.where(
            then >= begin2, begin3 - begin2, jnp.where(then >= begin1, begin2 - begin1, begin1 - begin0)
        )
        more = rest + AD
        wraps = more >= length
        agg_next = jnp.where(wraps, agg + 1, agg)
        rest_next = jnp.where(wraps, more - length, more)
        opens1 = then == begin1
        opens2 = then == begin2
        agg_next = jnp.where(opens1, AD, jnp.where(opens2, 2 * AD, agg_next))
        rest_next = jnp.where(opens1 | opens2, 0, rest_next)
        return jnp.where(moves, agg_next, agg), jnp.where(moves, rest_next, rest)

    lax.fori_loop(0, rows + 2 * W, step, (agg, rest))
    return begin1 - first


def scan_sent(count, table):
    def step(at, carry):
        off, end, begin, floor = carry
        opens = (at == 0) | (table[T_AGG + at + W] != table[T_AGG + jnp.maximum(at - 1, 0) + W])
        off = jnp.where(opens, end - table[T_AGG + at], off)
        begin = jnp.where(opens, end, begin)
        table[T_OFF + at] = off
        table[T_BASE + at] = begin
        end = off + table[T_AGG + at + 2 * W] + 1
        floor = jnp.where((at < W) | (begin < floor), end, floor)
        return off, end, begin, floor

    _, end, _, floor = lax.fori_loop(0, count, step, (0, 0, 0, 0))
    split = jnp.maximum(end - HALF, floor)

    def find(at, carry):
        low, high, begin = carry
        base = table[T_BASE + at]
        fresh = (base <= split) & (base != begin)
        low = jnp.where(fresh, at, low)
        begin = jnp.where(fresh, base, begin)
        high = jnp.where(base < split, at + 1, high)
        return low, high, begin

    low, high, _ = lax.fori_loop(0, count, find, (0, 0, -1))
    low = jnp.where(split >= end, count, low)
    return end, split, low, high


def one_row(row, group, valid, first, total, nbr, cnt, table, blocks, window):
    lowest = table[T_AGG + row] + NQ * group
    right = []
    left = []
    slots = blocks.shape[1]
    for k in range(slots):
        near = row + nbr[row, k]
        used = valid & (k < cnt[row]) & (first + near >= 0) & (first + near < total)
        at = jnp.where(used, table[T_AGG + near + W] - lowest, -1)
        value = window[near + W]
        zero = jnp.zeros_like(value)
        right.append(jnp.concatenate([jnp.where(at == q, value, zero) for q in range(NQ)], axis=1))
        left.append(blocks[row, k])
    applied = jnp.dot(
        jnp.concatenate(left, axis=1), jnp.concatenate(right, axis=0), preferred_element_type=jnp.float32
    ).astype(jnp.bfloat16)
    return lax.dot_general(
        window[row + W], applied, (((0,), (0,)), ((), ())), preferred_element_type=jnp.float32
    )


def all_rows(lo, hi, low_slot, high_slot, own, first, total, nbr, cnt, table, blocks, window, row_sems, a_hbm, acc):
    trash = acc.shape[0] - 1
    width = window.shape[2]

    def add(row, group, valid, term):
        agg = table[T_AGG + row + W]
        highest = table[T_AGG + row + 2 * W]
        off = (KC - 1) * agg - KC * AD + W if own else table[T_OFF + row]
        for q in range(NQ):
            target = table[T_AGG + row] + NQ * group + q
            slot = off + target
            ok = valid & (target <= highest) & (slot >= low_slot) & (slot < high_slot)
            at = jnp.where(ok, slot - low_slot, trash)
            acc[at] += term[:, q * width : (q + 1) * width]

    def block(step, carry):
        begin = lo + step * UNROLL
        for u in range(UNROLL):

            @pl.when(begin + u < hi)
            def _():
                row = begin + u
                pltpu.make_async_copy(a_hbm.at[row], blocks.at[row], row_sems.at[row]).wait()

        terms = []
        for u in range(UNROLL):
            valid = begin + u < hi
            row = jnp.minimum(begin + u, hi - 1)
            terms.append((row, valid, one_row(row, 0, valid, first, total, nbr, cnt, table, blocks, window)))
        for row, valid, term in terms:
            add(row, 0, valid, term)
        return carry

    lax.fori_loop(0, lax.div(hi - lo + UNROLL - 1, UNROLL), block, 0)

    def wide(row, carry):
        @pl.when(table[T_AGG + row + 2 * W] - table[T_AGG + row] >= NQ)
        def _():
            term = one_row(row, 1, True, first, total, nbr, cnt, table, blocks, window)
            add(row, 1, True, term)

        return carry

    lax.fori_loop(lo, hi, wide, 0)


def start_rows(lo, hi, a_hbm, blocks, row_sems):
    def step(row, carry):
        pltpu.make_async_copy(a_hbm.at[row], blocks.at[row], row_sems.at[row]).start()
        return carry

    lax.fori_loop(lo, hi, step, 0)


def clear(acc, count):
    def step(at, carry):
        acc[at] = jnp.zeros(acc.shape[1:], acc.dtype)
        return carry

    lax.fori_loop(0, count, step, 0)


def late_kernel(devices, pos_ref, own_ref, nbr, cnt, a_hbm, p_hbm, out, table, blocks, window, acc, sem, row_sems):
    rows = a_hbm.shape[0]
    pos = pos_ref[0]
    copy = pltpu.make_async_copy(p_hbm, window.at[pl.ds(W, rows)], sem)
    copy.start()
    count = scan_rows(pos, devices, rows, own_ref, table)
    end, split, low, high = scan_sent(count, table)
    start_rows(low, count, a_hbm, blocks, row_sems)
    table[T_N] = end
    table[T_H] = split
    table[T_LO] = low
    table[T_HI] = high
    table[T_S] = count
    clear(acc, HALF)
    copy.wait()
    all_rows(
        low, count, split, end, False, pos * rows, devices * rows, nbr, cnt, table, blocks, window, row_sems, a_hbm, acc
    )

    def give(at, carry):
        out[at] = acc[at].astype(out.dtype)
        return carry

    lax.fori_loop(0, HALF, give, 0)


def early_kernel(
    devices, pos_ref, own_ref, nbr, cnt, table, a_hbm, p_hbm, before, out, merge, blocks, window, acc, sem, sem2, row_sems
):
    rows = a_hbm.shape[0]
    pos = pos_ref[0]
    high = table[T_HI]
    copy = pltpu.make_async_copy(p_hbm, window.at[pl.ds(W, rows)], sem)
    copy.start()
    edge = pltpu.make_async_copy(before, window.at[pl.ds(0, W)], sem2)
    edge.start()
    start_rows(0, high, a_hbm, blocks, row_sems)
    clear(acc, HALF)
    copy.wait()
    edge.wait()
    all_rows(
        0, high, 0, table[T_H], False, pos * rows, devices * rows, nbr, cnt, table, blocks, window, row_sems, a_hbm, acc
    )

    def give(at, carry):
        out[at] = acc[at].astype(out.dtype)
        return carry

    lax.fori_loop(0, HALF, give, 0)

    count = jnp.where(
        pos + 1 < devices, scan_rows(pos + 1, devices, rows, own_ref, merge), 0
    )
    end, split, _, _ = scan_sent(count, merge)

    def place(row, done):
        agg = merge[T_AGG + row + W]

        def put(slot, carry):
            merge[T_DST + slot] = (KC - 1) * agg + W + slot - merge[T_OFF + row]
            return carry

        last = merge[T_OFF + row] + merge[T_AGG + row + 2 * W] + 1
        lax.fori_loop(done, last, put, 0)
        return last

    lax.fori_loop(0, count, place, 0)
    merge[T_N] = end
    merge[T_H] = split


def own_kernel(
    devices, pos_ref, nbr, cnt, table, order, a_hbm, p_hbm, before, after, out, blocks, window, acc, sem, sem2, sem3, sem4, row_sems
):
    rows = a_hbm.shape[0]
    pos = pos_ref[0]
    count = table[T_S]
    copy = pltpu.make_async_copy(p_hbm, window.at[pl.ds(W, rows)], sem)
    copy.start()
    edge = pltpu.make_async_copy(before, window.at[pl.ds(0, W)], sem2)
    edge.start()
    edge2 = pltpu.make_async_copy(after, window.at[pl.ds(W + rows, W)], sem3)
    edge2.start()
    start_rows(count, rows, a_hbm, blocks, row_sems)
    clear(acc, AD * KC)
    copy.wait()
    edge.wait()
    edge2.wait()
    all_rows(
        count, rows, 0, AD * KC, True, pos * rows, devices * rows, nbr, cnt, table, blocks, window, row_sems, a_hbm, acc
    )
    done = pltpu.make_async_copy(acc.at[pl.ds(0, AD * KC)], out, sem4)
    done.start()
    done.wait()


def merge_kernel(upper, merge, got, coarse, out, held, in_sems, out_sems):
    split = merge[T_H]
    begin = split if upper else 0
    count = merge[T_N] - split if upper else split

    def fetch(at):
        return pltpu.make_async_copy(coarse.at[merge[T_DST + begin + at]], held.at[at], in_sems.at[at])

    def store(at):
        return pltpu.make_async_copy(held.at[at], out.at[merge[T_DST + begin + at]], out_sems.at[at])

    def first(at, carry):
        fetch(at).start()
        return carry

    def second(at, carry):
        fetch(at).wait()
        held[at] += got[at].astype(jnp.float32)
        store(at).start()
        return carry

    def third(at, carry):
        store(at).wait()
        return carry

    lax.fori_loop(0, count, first, 0)
    lax.fori_loop(0, count, second, 0)
    lax.fori_loop(0, count, third, 0)


SMEM = pl.BlockSpec(memory_space=pltpu.SMEM)
VMEM = pl.BlockSpec(memory_space=pltpu.VMEM)
ANY = pl.BlockSpec(memory_space=pl.ANY)
DMA = pltpu.SemaphoreType.DMA


def params():
    return pltpu.CompilerParams(vmem_limit_bytes=50 * 1024 * 1024)


def cost(flops, moved):
    return pl.CostEstimate(flops=flops, bytes_accessed=moved, transcendentals=0)


def passed(block, step):
    devices = range(lax.axis_size(AXES))
    return lax.ppermute(block, AXES, [(i, i + step) for i in devices if i + step in devices])


def shards(a_blocks, nbr_offset, nbr_count, prolong, owner_start):
    devices = lax.axis_size(AXES)
    rows, slots, size, width = a_blocks.shape
    pos = lax.axis_index(AXES).reshape(1)
    flops = rows * slots * size * size * width * 2
    moved = rows * slots * size * width * 2
    work = [
        pltpu.VMEM((rows, slots, size, size), jnp.bfloat16),
        pltpu.VMEM((rows + 2 * W, size, width), jnp.bfloat16),
    ]
    table_shape = jax.ShapeDtypeStruct((T_LEN,), jnp.int32)
    sent_shape = jax.ShapeDtypeStruct((HALF, width, width), jnp.bfloat16)

    before = passed(prolong[rows - W :], 1)
    after = passed(prolong[:W], -1)
    late, table = pl.pallas_call(
        functools.partial(late_kernel, devices),
        out_shape=(sent_shape, table_shape),
        in_specs=[SMEM, SMEM, SMEM, SMEM, ANY, ANY],
        out_specs=(VMEM, SMEM),
        scratch_shapes=work
        + [pltpu.VMEM((HALF + 1, width, width), jnp.float32), DMA, DMA((rows,))],
        compiler_params=params(),
        cost_estimate=cost(flops // 2, moved // 2),
        name="late_rows",
    )(pos, owner_start, nbr_offset, nbr_count, a_blocks, prolong)
    got_late = passed(late, -1)
    early, merge = pl.pallas_call(
        functools.partial(early_kernel, devices),
        out_shape=(sent_shape, table_shape),
        in_specs=[SMEM, SMEM, SMEM, SMEM, SMEM, ANY, ANY, ANY],
        out_specs=(VMEM, SMEM),
        scratch_shapes=work
        + [pltpu.VMEM((HALF + 1, width, width), jnp.float32), DMA, DMA, DMA((rows,))],
        compiler_params=params(),
        cost_estimate=cost(flops // 2, moved // 2),
        name="early_rows",
    )(pos, owner_start, nbr_offset, nbr_count, table, a_blocks, prolong, before)
    got_early = passed(early, -1)
    coarse = pl.pallas_call(
        functools.partial(own_kernel, devices),
        out_shape=jax.ShapeDtypeStruct((AD * KC, width, width), jnp.float32),
        in_specs=[SMEM, SMEM, SMEM, SMEM, SMEM, ANY, ANY, ANY, ANY],
        out_specs=ANY,
        scratch_shapes=work
        + [pltpu.VMEM((AD * KC + 1, width, width), jnp.float32), DMA, DMA, DMA, DMA, DMA((rows,))],
        compiler_params=params(),
        cost_estimate=cost(flops, moved),
        name="own_rows",
    )(pos, nbr_offset, nbr_count, table, merge, a_blocks, prolong, before, after)
    for upper, got in ((True, got_late), (False, got_early)):
        coarse = pl.pallas_call(
            functools.partial(merge_kernel, upper),
            out_shape=jax.ShapeDtypeStruct(coarse.shape, coarse.dtype),
            in_specs=[SMEM, VMEM, ANY],
            out_specs=ANY,
            scratch_shapes=[
                pltpu.VMEM((HALF, width, width), jnp.float32),
                DMA((HALF,)),
                DMA((HALF,)),
            ],
            input_output_aliases={2: 0},
            compiler_params=params(),
            name="merge_late" if upper else "merge_early",
        )(merge, got, coarse)
    return coarse.reshape(AD, KC, width, width)


def solution(mesh):
    placed = (
        P(("dom", "sub"), None, None, None),
        P(("dom", "sub"), None),
        P(("dom", "sub")),
        P(("dom", "sub"), None, None),
        P(),
    )
    return jax.shard_map(
        shards,
        mesh=mesh,
        in_specs=placed,
        out_specs=P(("dom", "sub"), None, None, None),
        check_vma=False,
    )
```

```python
import functools

import jax
import jax.numpy as jnp
from jax import lax
from jax.experimental import pallas as pl
from jax.experimental.pallas import tpu as pltpu
from jax.sharding import PartitionSpec as P

W = 3
KC = 7
AD = 16
SMAX = 48
NQ = 4
UNROLL = 4
HALF = 22
AXES = ("dom", "sub")

QUOTA = 24

T_AGG = 0
T_OFF = 128
T_BASE = 256
T_DST = 384
T_N = 448
T_H = 449
T_LO = 450
T_HI = 451
T_S = 452
T_OWN0 = 453
T_OWN1 = 454
T_OWN2 = 455
T_LAST = 456
T_LEN = 512


def scan_rows(pos, devices, rows, own_ref, table):
    def start(owner):
        inside = (owner >= 0) & (owner < devices)
        at = jnp.clip(owner, 0, devices - 1)
        return jnp.where(inside, own_ref[at], jnp.where(owner < 0, 0, devices * rows))

    total = devices * rows
    first = pos * rows
    begin0, begin1, begin2, begin3 = (start(pos - 1), start(pos), start(pos + 1), start(pos + 2))
    row = jnp.maximum(first - W, 0)
    below = row < begin1
    length = jnp.maximum(jnp.where(below, begin1 - begin0, begin2 - begin1), 1)
    scaled = (row - jnp.where(below, begin0, begin1)) * AD
    local = lax.div(scaled, length)
    agg = jnp.where(below, 0, AD) + local
    rest = scaled - local * length

    def step(at, carry):
        agg, rest = carry
        table[T_AGG + at] = agg
        here = first + at - W
        moves = (here >= 0) & (here < total - 1)
        then = here + 1
        length = jnp.where(
            then >= begin2, begin3 - begin2, jnp.where(then >= begin1, begin2 - begin1, begin1 - begin0)
        )
        more = rest + AD
        wraps = more >= length
        agg_next = jnp.where(wraps, agg + 1, agg)
        rest_next = jnp.where(wraps, more - length, more)
        opens1 = then == begin1
        opens2 = then == begin2
        agg_next = jnp.where(opens1, AD, jnp.where(opens2, 2 * AD, agg_next))
        rest_next = jnp.where(opens1 | opens2, 0, rest_next)
        return jnp.where(moves, agg_next, agg), jnp.where(moves, rest_next, rest)

    lax.fori_loop(0, rows + 2 * W, step, (agg, rest))
    return begin1 - first


def scan_sent(count, table):
    def step(at, carry):
        off, end, begin, floor, even = carry
        opens = (at == 0) | (table[T_AGG + at + W] != table[T_AGG + jnp.maximum(at - 1, 0) + W])
        off = jnp.where(opens, end - table[T_AGG + at], off)
        begin = jnp.where(opens, end, begin)
        table[T_OFF + at] = off
        table[T_BASE + at] = begin
        end = off + table[T_AGG + at + 2 * W] + 1
        floor = jnp.where((at < W) | (begin < floor), end, floor)
        even = jnp.where((at < count - QUOTA) | (begin < even), end, even)
        return off, end, begin, floor, even

    _, end, _, floor, even = lax.fori_loop(0, count, step, (0, 0, 0, 0, 0))
    split = jnp.maximum(jnp.maximum(end - HALF, floor), jnp.minimum(even, HALF))

    def find(at, carry):
        low, high, begin = carry
        base = table[T_BASE + at]
        fresh = (base <= split) & (base != begin)
        low = jnp.where(fresh, at, low)
        begin = jnp.where(fresh, base, begin)
        high = jnp.where(base < split, at + 1, high)
        return low, high, begin

    low, high, _ = lax.fori_loop(0, count, find, (0, 0, -1))
    low = jnp.where(split >= end, count, low)
    return end, split, low, high


def share_own(rows, count, low, high, table):
    first = jnp.maximum(QUOTA - (count - low), 0)
    second = jnp.maximum(QUOTA - high, 0)

    def step(row, carry):
        own0, own1, own2 = carry
        opens = (row == count) | (table[T_AGG + row + W] != table[T_AGG + row + W - 1])
        fresh = opens & (row >= W) & (own0 < 0)
        own0 = jnp.where(fresh, row, own0)
        own1 = jnp.where(fresh, row, own1)
        own2 = jnp.where(fresh, row, own2)
        inside = opens & (own0 >= 0) & (row <= rows - W)
        own1 = jnp.where(inside & (row <= own0 + first), row, own1)
        own2 = jnp.where(inside & (row <= own1 + second), row, own2)
        return own0, own1, own2

    return lax.fori_loop(count, rows, step, (-1, -1, -1))


def place_of(row, k, group, valid, first, total, nbr, cnt, table):
    near = row + nbr[k, row]
    used = valid & (k < cnt[row]) & (first + near >= 0) & (first + near < total)
    column = table[T_AGG + near + W] - table[T_AGG + row] - NQ * group
    return near + W, jnp.where(used & (column >= 0) & (column < NQ), column, NQ)


def apply_row(row, group, valid, first, total, nbr, cnt, table, blocks, window, sums):
    width = window.shape[2]
    for k in range(0, blocks.shape[1], 2):
        at0, q0 = place_of(row, k, group, valid, first, total, nbr, cnt, table)
        at1, q1 = place_of(row, k + 1, group, valid, first, total, nbr, cnt, table)
        near0, near1 = window[at0], window[at1]
        zero = jnp.zeros_like(near0)
        right = jnp.concatenate(
            [jnp.concatenate([near0, zero], axis=1), jnp.concatenate([zero, near1], axis=1)], axis=0
        )
        left = jnp.concatenate([blocks[row, k], blocks[row, k + 1]], axis=1)
        product = jnp.dot(left, right, preferred_element_type=jnp.float32)
        sums[q0] += product[:, :width]
        sums[q1] += product[:, width:]


def round_row(sums, applied):
    width = sums.shape[2]
    for q in range(NQ):
        applied[:, q * width : (q + 1) * width] = sums[q].astype(applied.dtype)
        sums[q] = jnp.zeros(sums.shape[1:], sums.dtype)


def all_rows(ranges, low_slot, high_slot, first, total, nbr, cnt, table, blocks, window, sums, applied, row_sems, a_hbm, acc):
    (lo0, hi0), (lo1, hi1) = ranges
    width = window.shape[2]
    count = table[T_S]
    turn = hi0 - lo0
    amount = turn + hi1 - lo1

    def row_at(index):
        return jnp.where(index < turn, lo0 + index, lo1 + index - turn)

    def start(index, carry):
        row = row_at(index)
        pltpu.make_async_copy(a_hbm.at[row], blocks.at[row], row_sems.at[row]).start()
        return carry

    def add(row, group, valid, u):
        term = lax.dot_general(
            window[row + W], applied[u][...], (((0,), (0,)), ((), ())), preferred_element_type=jnp.float32
        )
        agg = table[T_AGG + row + W]
        highest = table[T_AGG + row + 2 * W]
        own = row >= count
        for q in range(NQ):
            target = table[T_AGG + row] + NQ * group + q
            sent = table[T_OFF + row] + target
            kept = (KC - 1) * agg - KC * AD + W + target
            ok = valid & (target <= highest) & (own | ((sent >= low_slot) & (sent < high_slot)))
            at = jnp.where(ok, jnp.where(own, HALF + 1 + kept, sent - low_slot), HALF)
            acc[at] += term[:, q * width : (q + 1) * width]

    def add_block(begin):
        for u in range(UNROLL):
            index = begin + u
            row = row_at(jnp.clip(index, 0, amount - 1))
            add(row, 0, (index >= 0) & (index < amount), u)

    def block(step, carry):
        begin = step * UNROLL
        for u in range(UNROLL):

            @pl.when(begin + u < amount)
            def _():
                row = row_at(begin + u)
                pltpu.make_async_copy(a_hbm.at[row], blocks.at[row], row_sems.at[row]).wait()

        add_block(begin - UNROLL)
        for u in range(UNROLL):
            row = row_at(jnp.minimum(begin + u, amount - 1))
            apply_row(row, 0, begin + u < amount, first, total, nbr, cnt, table, blocks, window, sums[u])
        for u in range(UNROLL):
            round_row(sums[u], applied[u])
        return carry

    def run():
        for u in range(UNROLL):
            for q in range(NQ):
                sums[u][q] = jnp.zeros(sums[u].shape[1:], sums[u].dtype)

        @pl.when(amount > 0)
        def _():
            steps = lax.div(amount + UNROLL - 1, UNROLL)
            lax.fori_loop(0, steps, block, 0)
            add_block((steps - 1) * UNROLL)

            def wide(index, carry):
                row = row_at(index)

                @pl.when(table[T_AGG + row + 2 * W] - table[T_AGG + row] >= NQ)
                def _():
                    apply_row(row, 1, True, first, total, nbr, cnt, table, blocks, window, sums[0])
                    round_row(sums[0], applied[0])
                    add(row, 1, True, 0)

                return carry

            lax.fori_loop(0, amount, wide, 0)

    lax.fori_loop(0, amount, start, 0)
    return run


def clear(acc, begin, end):
    def step(at, carry):
        acc[at] = jnp.zeros(acc.shape[1:], acc.dtype)
        return carry

    lax.fori_loop(begin, end, step, 0)


def give(acc, out):
    def step(at, carry):
        out[at] = acc[at].astype(out.dtype)
        return carry

    lax.fori_loop(0, HALF, step, 0)


def write_own(begin, end, acc, coarse, sems):
    def copy(agg):
        return pltpu.make_async_copy(
            acc.at[pl.ds(HALF + 1 + agg * KC, KC)], coarse.at[pl.ds(agg * KC, KC)], sems.at[agg]
        )

    def start(agg, carry):
        copy(agg).start()
        return carry

    def wait(agg, carry):
        copy(agg).wait()
        return carry

    lax.fori_loop(begin, end, start, 0)
    return lambda: lax.fori_loop(begin, end, wait, 0)


def position():
    place = 0
    for axis in AXES:
        place = place * lax.axis_size(axis) + lax.axis_index(axis)
    return place


def late_kernel(
    devices, own_hbm, nbr_hbm, cnt_hbm, a_hbm, p_hbm, out, coarse, table, nbr, cnt, own, blocks, window, sums, applied, acc, sems, row_sems, out_sems
):
    rows = a_hbm.shape[0]
    pos = position()
    copies = [
        pltpu.make_async_copy(own_hbm, own, sems.at[0]),
        pltpu.make_async_copy(nbr_hbm, nbr, sems.at[1]),
        pltpu.make_async_copy(cnt_hbm, cnt, sems.at[2]),
        pltpu.make_async_copy(p_hbm, window.at[pl.ds(W, rows)], sems.at[3]),
    ]
    for copy in copies:
        copy.start()
    copies[0].wait()
    count = scan_rows(pos, devices, rows, own, table)
    end, split, low, high = scan_sent(count, table)
    own0, own1, own2 = share_own(rows, count, low, high, table)
    table[T_N] = end
    table[T_H] = split
    table[T_LO] = low
    table[T_HI] = high
    table[T_S] = count
    table[T_OWN0] = own0
    table[T_OWN1] = own1
    table[T_OWN2] = own2
    table[T_LAST] = table[T_AGG + rows - 1 + W] - AD
    run = all_rows(
        ((low, count), (own0, own1)), split, end, pos * rows, devices * rows, nbr, cnt, table, blocks, window, sums, applied, row_sems, a_hbm, acc
    )
    begin = table[T_AGG + own0 + W] - AD
    stop = table[T_AGG + own1 + W] - AD
    clear(acc, 0, HALF)
    clear(acc, HALF + 1 + begin * KC, HALF + 1 + stop * KC)
    for copy in copies[1:]:
        copy.wait()
    for at in range(W):
        out[HALF + at] = window[W + at]
    run()
    finish = write_own(begin, stop, acc, coarse, out_sems)
    give(acc, out)
    finish()


def early_kernel(
    devices, own_hbm, nbr, cnt, table, a_hbm, p_hbm, before, _, out, coarse, merge, own, blocks, window, sums, applied, acc, sems, row_sems, out_sems
):
    rows = a_hbm.shape[0]
    pos = position()
    own1, own2 = table[T_OWN1], table[T_OWN2]
    copies = [
        pltpu.make_async_copy(own_hbm, own, sems.at[0]),
        pltpu.make_async_copy(p_hbm, window.at[pl.ds(W, rows)], sems.at[1]),
        pltpu.make_async_copy(before, window.at[pl.ds(0, W)], sems.at[2]),
    ]
    for copy in copies:
        copy.start()
    run = all_rows(
        ((0, table[T_HI]), (own1, own2)), 0, table[T_H], pos * rows, devices * rows, nbr, cnt, table, blocks, window, sums, applied, row_sems, a_hbm, acc
    )
    begin = table[T_AGG + own1 + W] - AD
    stop = table[T_AGG + own2 + W] - AD
    clear(acc, 0, HALF)
    clear(acc, HALF + 1 + begin * KC, HALF + 1 + stop * KC)
    for copy in copies:
        copy.wait()
    run()
    finish = write_own(begin, stop, acc, coarse, out_sems)
    give(acc, out)

    count = jnp.where(pos + 1 < devices, scan_rows(pos + 1, devices, rows, own, merge), 0)
    end, split, _, _ = scan_sent(count, merge)

    def place(row, done):
        agg = merge[T_AGG + row + W]

        def put(slot, carry):
            merge[T_DST + slot] = (KC - 1) * agg + W + slot - merge[T_OFF + row]
            return carry

        last = merge[T_OFF + row] + merge[T_AGG + row + 2 * W] + 1
        lax.fori_loop(done, last, put, 0)
        return last

    lax.fori_loop(0, count, place, 0)
    merge[T_N] = end
    merge[T_H] = split
    finish()


def own_kernel(
    devices, nbr, cnt, table, merge, a_hbm, p_hbm, before, got, _, coarse, edge, blocks, window, sums, applied, acc, sems, row_sems, out_sems
):
    rows = a_hbm.shape[0]
    pos = position()
    count, own0, own2 = table[T_S], table[T_OWN0], table[T_OWN2]
    copies = [
        pltpu.make_async_copy(p_hbm, window.at[pl.ds(W, rows)], sems.at[0]),
        pltpu.make_async_copy(before, window.at[pl.ds(0, W)], sems.at[1]),
    ]
    for copy in copies:
        copy.start()
    run = all_rows(
        ((count, own0), (own2, rows)), 0, 0, pos * rows, devices * rows, nbr, cnt, table, blocks, window, sums, applied, row_sems, a_hbm, acc
    )
    skip = table[T_AGG + own0 + W] - AD
    resume = table[T_AGG + own2 + W] - AD
    clear(acc, HALF + 1, HALF + 1 + skip * KC)
    clear(acc, HALF + 1 + resume * KC, HALF + 1 + AD * KC)
    for at in range(W):
        window[W + rows + at] = got[HALF + at]
    for copy in copies:
        copy.wait()
    run()
    split = merge[T_H]

    def add(slot, carry):
        acc[HALF + 1 + merge[T_DST + slot]] += got[slot - split].astype(jnp.float32)
        return carry

    lax.fori_loop(split, merge[T_N], add, 0)
    finish0 = write_own(0, skip, acc, coarse, out_sems)
    finish1 = write_own(resume, AD, acc, coarse, out_sems)
    last = table[T_LAST]
    for at in range(KC):
        edge[at] = acc[HALF + 1 + last * KC + at]
    finish0()
    finish1()


def merge_kernel(table, merge, got, edge, _, coarse, held, sems):
    last = table[T_LAST] * KC
    split = merge[T_H]

    def store(slot):
        return pltpu.make_async_copy(held.at[slot], coarse.at[merge[T_DST + slot]], sems.at[slot])

    def start(slot, carry):
        at = merge[T_DST + slot] - last
        shared = (at >= 0) & (at < KC)
        base = edge[jnp.clip(at, 0, KC - 1)]
        held[slot] = got[slot].astype(jnp.float32) + jnp.where(shared, base, jnp.zeros_like(base))
        store(slot).start()
        return carry

    def wait(slot, carry):
        store(slot).wait()
        return carry

    lax.fori_loop(0, split, start, 0)
    lax.fori_loop(0, split, wait, 0)


SMEM = pl.BlockSpec(memory_space=pltpu.SMEM)
VMEM = pl.BlockSpec(memory_space=pltpu.VMEM)
HBM = pl.BlockSpec(memory_space=pltpu.HBM)
DMA = pltpu.SemaphoreType.DMA


def params():
    return pltpu.CompilerParams(vmem_limit_bytes=50 * 1024 * 1024)


def cost(flops, moved):
    return pl.CostEstimate(flops=flops, bytes_accessed=moved, transcendentals=0)


def passed(block, step):
    devices = range(lax.axis_size(AXES))
    return lax.ppermute(block, AXES, [(i, i + step) for i in devices if i + step in devices])


def shards(a_blocks, nbr_offset, nbr_count, prolong, owner_start):
    devices = lax.axis_size(AXES)
    rows, slots, size, width = a_blocks.shape
    flops = rows * slots * size * size * width * 2
    moved = rows * slots * size * width * 2
    work = [
        pltpu.VMEM((rows, slots, size, size), jnp.bfloat16),
        pltpu.VMEM((rows + 2 * W, size, width), jnp.bfloat16),
        [pltpu.VMEM((NQ + 1, size, width), jnp.float32)] * UNROLL,
        [pltpu.VMEM((size, NQ * width), jnp.bfloat16)] * UNROLL,
        pltpu.VMEM((HALF + 1 + AD * KC, width, width), jnp.float32),
        DMA((4,)),
        DMA((rows,)),
        DMA((AD,)),
    ]
    numbers = pltpu.SMEM(owner_start.shape, jnp.int32)
    table_shape = jax.ShapeDtypeStruct((T_LEN,), jnp.int32)
    coarse_shape = jax.ShapeDtypeStruct((AD * KC, width, width), jnp.float32)
    offsets = nbr_offset.T

    before = passed(prolong[rows - W :], 1)
    late, coarse, table, nbr, cnt = pl.pallas_call(
        functools.partial(late_kernel, devices),
        out_shape=(
            jax.ShapeDtypeStruct((HALF + W, width, width), jnp.bfloat16),
            coarse_shape,
            table_shape,
            jax.ShapeDtypeStruct(offsets.shape, jnp.int32),
            jax.ShapeDtypeStruct(nbr_count.shape, jnp.int32),
        ),
        in_specs=[HBM] * 5,
        out_specs=(VMEM, HBM, SMEM, SMEM, SMEM),
        scratch_shapes=[numbers] + work,
        compiler_params=params(),
        cost_estimate=cost(flops // 3, moved // 3),
        name="late_rows",
    )(owner_start, offsets, nbr_count, a_blocks, prolong)
    got_late = passed(late, -1)
    early, coarse, merge = pl.pallas_call(
        functools.partial(early_kernel, devices),
        out_shape=(jax.ShapeDtypeStruct((HALF, width, width), jnp.bfloat16), coarse_shape, table_shape),
        in_specs=[HBM, SMEM, SMEM, SMEM, HBM, HBM, HBM, HBM],
        out_specs=(VMEM, HBM, SMEM),
        scratch_shapes=[numbers] + work,
        input_output_aliases={7: 1},
        compiler_params=params(),
        cost_estimate=cost(flops // 3, moved // 3),
        name="early_rows",
    )(owner_start, nbr, cnt, table, a_blocks, prolong, before, coarse)
    got_early = passed(early, -1)
    coarse, edge = pl.pallas_call(
        functools.partial(own_kernel, devices),
        out_shape=(coarse_shape, jax.ShapeDtypeStruct((KC, width, width), jnp.float32)),
        in_specs=[SMEM] * 4 + [HBM] * 3 + [VMEM, HBM],
        out_specs=(HBM, VMEM),
        scratch_shapes=work,
        input_output_aliases={8: 0},
        compiler_params=params(),
        cost_estimate=cost(flops // 3, moved // 3),
        name="own_rows",
    )(nbr, cnt, table, merge, a_blocks, prolong, before, got_late, coarse)
    coarse = pl.pallas_call(
        merge_kernel,
        out_shape=coarse_shape,
        in_specs=[SMEM, SMEM, VMEM, VMEM, HBM],
        out_specs=HBM,
        scratch_shapes=[pltpu.VMEM((HALF, width, width), jnp.float32), DMA((HALF,))],
        input_output_aliases={4: 0},
        compiler_params=params(),
        name="merge_rows",
    )(table, merge, got_early, edge, coarse)
    return coarse.reshape(AD, KC, width, width)


def solution(mesh):
    placed = (
        P(("dom", "sub"), None, None, None),
        P(("dom", "sub"), None),
        P(("dom", "sub")),
        P(("dom", "sub"), None, None),
        P(),
    )
    return jax.shard_map(
        shards,
        mesh=mesh,
        in_specs=placed,
        out_specs=P(("dom", "sub"), None, None, None),
        check_vma=False,
    )
```

```python
import functools

import jax
import jax.numpy as jnp
from jax import lax
from jax.experimental import pallas as pl
from jax.experimental.pallas import tpu as pltpu
from jax.sharding import PartitionSpec as P

W = 3
KC = 7
AD = 16
SMAX = 48
NQ = 2
UNROLL = 6
HALF = 22
AXES = ("dom", "sub")


AHEAD = 16
SHIFT = 20
FAR = 1024

T_AGG = 0
T_OFF = 128
T_BASE = 192
T_ROW = 256
T_DST = 384
T_CUM = 512
T_COLUMN = 640
T_N = 448
T_H = 449
T_LO = 450
T_HI = 451
T_S = 452
T_OWN0 = 453
T_OWN1 = 454
T_OWN2 = 455
T_LAST = 456
T_NEXT = 457
T_GROUP = 128
T_LEN = 768


def starts(pos, devices, rows, own_ref):
    def start(owner):
        at = jnp.clip(owner, 0, devices - 1)
        given = jnp.where(owner < devices, own_ref[at], devices * rows)
        return jnp.where(owner < 0, 0, given) - pos * rows

    return [start(pos + step) for step in (-1, 0, 1, 2)]


def row_start(begin, length, agg):
    return begin + lax.shift_right_logical(agg * length + (AD - 1), 4)


def scan_rows(pos, devices, rows, begins, table):
    total = devices * rows
    first = pos * rows
    scale = []
    for owner in range(3):
        length = jnp.maximum(begins[owner + 1] - begins[owner], 1)
        scale.append(lax.div(length + (2**SHIFT - 1), length) * AD)
    items = jnp.int32(0)
    aggs = []
    for at in range(rows + 2 * W):
        row = at - W

        def local(owner):
            return lax.shift_right_logical((row - begins[owner]) * scale[owner], SHIFT) + owner * AD

        if row >= rows:
            agg = jnp.where(row >= begins[2], local(2), local(1))
            agg = jnp.where(first + row < total, agg, aggs[-1])
            column = jnp.where(first + row < total, agg, FAR)
        elif row >= SMAX:
            agg = column = local(1)
        elif row >= 0:
            agg = column = jnp.where(row >= begins[1], local(1), local(0))
        else:
            agg = jnp.where(first > 0, local(0), AD)
            column = jnp.where(first > 0, agg, FAR)
        aggs.append(agg)
        table[T_AGG + at] = agg
        table[T_COLUMN + at] = column
        if at >= 2 * W:
            table[T_CUM + at - 2 * W] = items
            items = items + (lax.shift_right_logical(agg - aggs[at - 2 * W], 1) + 1)
    table[T_CUM + rows] = items


def scan_sent(rows, begins, table, places):
    count = begins[1]
    length = begins[1] - begins[0]
    sent = table[T_CUM + count]
    share = jnp.maximum(lax.div(3 * table[T_CUM + rows], 8), lax.div(sent + 1, 2))
    lowest = jnp.where(count > 0, table[T_AGG + W], AD)

    def span(agg):
        return (
            jnp.maximum(row_start(begins[0], length, agg), 0),
            jnp.minimum(row_start(begins[0], length, agg + 1), count),
        )

    def step(agg, carry):
        end, floor, even = carry
        row, stop = span(agg)
        off = end - table[T_AGG + row]
        table[T_OFF + agg] = off
        table[T_BASE + agg] = end
        table[T_ROW + agg] = row
        begin = end
        end = off + table[T_AGG + stop - 1 + 2 * W] + 1
        if places:

            def put(slot, carry):
                table[T_DST + slot] = (KC - 1) * agg + W + slot - off
                return carry

            lax.fori_loop(begin, end, put, 0)
        floor = jnp.where(row < W, end, floor)
        even = jnp.where(sent - table[T_CUM + row] > share, end, even)
        return end, floor, even

    end, floor, even = lax.fori_loop(lowest, AD, step, (0, 0, 0))
    split = jnp.maximum(jnp.maximum(end - HALF, floor), jnp.minimum(even, HALF))
    table[T_N] = end
    table[T_H] = split
    if places:
        return

    def find(agg, carry):
        low, high = carry
        base = table[T_BASE + agg]
        row, stop = span(agg)
        low = jnp.where(base <= split, row, low)
        high = jnp.where(base < split, stop, high)
        return low, high

    low, high = lax.fori_loop(lowest, AD, find, (0, 0))
    table[T_LO] = jnp.where(split >= end, count, low)
    table[T_HI] = high


def share_own(rows, begins, table):
    count = begins[1]
    length = begins[2] - begins[1]
    share = lax.div(3 * table[T_CUM + rows], 8)
    first = jnp.maximum(share - table[T_CUM + count] + table[T_CUM + table[T_LO]], 0)
    second = jnp.maximum(share - table[T_CUM + table[T_HI]], 0)

    def step(agg, carry):
        own0, own1, own2 = carry
        row = row_start(count, length, agg)
        fresh = (row >= W) & (own0 < 0)
        own0 = jnp.where(fresh, row, own0)
        own1 = jnp.where(fresh, row, own1)
        own2 = jnp.where(fresh, row, own2)
        inside = (own0 >= 0) & (row <= rows - W)
        done = table[T_CUM + row]
        own1 = jnp.where(inside & (done <= table[T_CUM + jnp.maximum(own0, 0)] + first), row, own1)
        own2 = jnp.where(inside & (done <= table[T_CUM + jnp.maximum(own1, 0)] + second), row, own2)
        return own0, own1, own2

    own0, own1, own2 = lax.fori_loop(0, AD, step, (-1, -1, -1))
    table[T_OWN0] = own0
    table[T_OWN1] = own1
    table[T_OWN2] = own2
    table[T_S] = count
    table[T_LAST] = table[T_AGG + rows - 1 + W] - AD


def apply_row(row, group, nbr, cnt, table, blocks, window, applied):
    right = []
    left = []
    slots = cnt[row]
    lowest = table[T_AGG + row] + NQ * group
    for k in range(blocks.shape[1]):
        at = row + W + nbr[k, row]
        near = window[at]
        column = jnp.where(k < slots, table[T_COLUMN + at], FAR) - lowest
        zero = jnp.zeros_like(near)
        right.append(jnp.concatenate([jnp.where(column == q, near, zero) for q in range(NQ)], axis=1))
        left.append(blocks[row, k])
    applied[...] = jnp.dot(
        jnp.concatenate(left, axis=1), jnp.concatenate(right, axis=0), preferred_element_type=jnp.float32
    ).astype(applied.dtype)


def all_rows(ranges, ahead, low_slot, high_slot, nbr, cnt, table, blocks, window, applied, turned, items, row_sems, a_hbm, acc):
    (lo0, hi0), (lo1, hi1) = ranges
    width = window.shape[2]
    count = table[T_S]
    turn = hi0 - lo0

    def row_at(index):
        return jnp.where(index < turn, lo0 + index, lo1 + index - turn)

    def start(index, amount):
        row = row_at(index)

        @pl.when((row < ahead) | (row >= count))
        def _():
            pltpu.make_async_copy(a_hbm.at[row], blocks.at[row], row_sems.at[row]).start()

        for group in range((2 * W) // NQ + 1):
            items[amount + group] = row + T_GROUP * group
        return amount + table[T_CUM + row + 1] - table[T_CUM + row]

    amount = lax.fori_loop(0, turn + hi1 - lo1, start, 0)

    def item(index):
        at = items[jnp.clip(index, 0, amount - 1)]
        valid = (index >= 0) & (index < amount)
        return at & (T_GROUP - 1), lax.shift_right_logical(at, 7), valid

    def add(row, group, valid, u):
        term = jnp.dot(turned[u][...], applied[u][...], preferred_element_type=jnp.float32)
        agg = table[T_AGG + row + W]
        highest = table[T_AGG + row + 2 * W]
        own = row >= count
        for q in range(NQ):
            target = table[T_AGG + row] + NQ * group + q
            sent = table[T_OFF + agg] + target
            kept = (KC - 1) * agg - KC * AD + W + target
            ok = valid & (target <= highest) & (own | ((sent >= low_slot) & (sent < high_slot)))
            at = jnp.where(ok, jnp.where(own, HALF + 1 + kept, sent - low_slot), HALF)
            acc[at] += term[:, q * width : (q + 1) * width]

    def add_block(begin):
        for u in range(UNROLL):
            row, group, valid = item(begin + u)
            add(row, group, valid, u)

    def block(step, carry):
        begin = step * UNROLL
        for u in range(UNROLL):
            row, group, valid = item(begin + u)

            @pl.when(valid & (group == 0))
            def _():
                pltpu.make_async_copy(a_hbm.at[row], blocks.at[row], row_sems.at[row]).wait()

        add_block(begin - UNROLL)
        for u in range(UNROLL):
            row, group, valid = item(begin + u)
            apply_row(row, group, nbr, cnt, table, blocks, window, applied[u])
            turned[u][...] = window[row + W].T
        return carry

    def run():
        @pl.when(amount > 0)
        def _():
            steps = lax.div(amount + UNROLL - 1, UNROLL)
            lax.fori_loop(0, steps, block, 0)
            add_block((steps - 1) * UNROLL)

    return run


def clear(acc, begin, end):
    def step(at, carry):
        acc[at] = jnp.zeros(acc.shape[1:], acc.dtype)
        return carry

    lax.fori_loop(begin, end, step, 0)


def give(acc, out):
    def step(at, carry):
        out[at] = acc[at].astype(out.dtype)
        return carry

    lax.fori_loop(0, HALF, step, 0)


def write_own(begin, end, acc, coarse, sems):
    def copy(agg):
        return pltpu.make_async_copy(
            acc.at[pl.ds(HALF + 1 + agg * KC, KC)], coarse.at[pl.ds(agg * KC, KC)], sems.at[agg]
        )

    def start(agg, carry):
        copy(agg).start()
        return carry

    def wait(agg, carry):
        copy(agg).wait()
        return carry

    lax.fori_loop(begin, end, start, 0)
    return lambda: lax.fori_loop(begin, end, wait, 0)


def position():
    place = 0
    for axis in AXES:
        place = place * lax.axis_size(axis) + lax.axis_index(axis)
    return place


def late_kernel(
    devices, own_hbm, nbr_hbm, cnt_hbm, a_hbm, p_hbm, out, tail, coarse, table, own, nbr, cnt, blocks, window, applied, turned, items, acc, sems, row_sems, out_sems
):
    rows = a_hbm.shape[0]
    pos = position()
    copies = [
        pltpu.make_async_copy(own_hbm, own, sems.at[0]),
        pltpu.make_async_copy(nbr_hbm, nbr, sems.at[1]),
        pltpu.make_async_copy(cnt_hbm, cnt, sems.at[2]),
        pltpu.make_async_copy(p_hbm, window.at[pl.ds(W, rows)], sems.at[3]),
    ]
    for copy in copies:
        copy.start()
    copies[0].wait()
    begins = starts(pos, devices, rows, own)
    for at, begin in enumerate(starts(pos + 1, devices, rows, own)):
        table[T_NEXT + at] = begin
    count = begins[1]
    ahead = jnp.maximum(count - AHEAD, W)

    def fetch(row):
        return pltpu.make_async_copy(a_hbm.at[row], blocks.at[row], row_sems.at[row])

    def prefetch(row, carry):
        fetch(row).start()
        return carry

    def drain(row, carry):
        fetch(row).wait()
        return carry

    lax.fori_loop(ahead, count, prefetch, 0)
    scan_rows(pos, devices, rows, begins, table)
    scan_sent(rows, begins, table, False)
    share_own(rows, begins, table)
    low, own0, own1 = table[T_LO], table[T_OWN0], table[T_OWN1]
    run = all_rows(
        ((low, count), (own0, own1)), ahead, table[T_H], table[T_N], nbr, cnt, table, blocks, window, applied, turned, items, row_sems, a_hbm, acc
    )
    begin = table[T_AGG + own0 + W] - AD
    stop = table[T_AGG + own1 + W] - AD
    clear(acc, 0, HALF)
    clear(acc, HALF + 1 + begin * KC, HALF + 1 + stop * KC)
    copies[1].wait()
    copies[2].wait()
    copies[3].wait()
    for at in range(W):
        out[HALF + at] = window[W + at]
        tail[at] = window[rows + at]
    run()
    finish = write_own(begin, stop, acc, coarse, out_sems)
    give(acc, out)
    lax.fori_loop(ahead, low, drain, 0)
    finish()


def early_kernel(
    devices, table, nbr_hbm, cnt_hbm, a_hbm, p_hbm, before, _, out, coarse, nbr, cnt, blocks, window, applied, turned, items, acc, sems, row_sems, out_sems
):
    rows = a_hbm.shape[0]
    pos = position()
    own1, own2 = table[T_OWN1], table[T_OWN2]
    copies = [
        pltpu.make_async_copy(p_hbm, window.at[pl.ds(W, rows)], sems.at[0]),
        pltpu.make_async_copy(before, window.at[pl.ds(0, W)], sems.at[1]),
        pltpu.make_async_copy(nbr_hbm, nbr, sems.at[2]),
        pltpu.make_async_copy(cnt_hbm, cnt, sems.at[3]),
    ]
    for copy in copies:
        copy.start()
    run = all_rows(
        ((0, table[T_HI]), (own1, own2)), table[T_S], 0, table[T_H], nbr, cnt, table, blocks, window, applied, turned, items, row_sems, a_hbm, acc
    )
    begin = table[T_AGG + own1 + W] - AD
    stop = table[T_AGG + own2 + W] - AD
    clear(acc, 0, HALF)
    clear(acc, HALF + 1 + begin * KC, HALF + 1 + stop * KC)
    copies[2].wait()
    copies[3].wait()
    copies[0].wait()
    copies[1].wait()
    run()
    finish = write_own(begin, stop, acc, coarse, out_sems)
    give(acc, out)
    finish()


def own_kernel(
    devices, table, nbr_hbm, cnt_hbm, a_hbm, p_hbm, before, got, _, coarse, merge, nbr, cnt, blocks, window, applied, turned, items, acc, sems, row_sems, out_sems
):
    rows = a_hbm.shape[0]
    pos = position()
    count, own0, own2, last = table[T_S], table[T_OWN0], table[T_OWN2], table[T_LAST]
    copies = [
        pltpu.make_async_copy(p_hbm, window.at[pl.ds(W, rows)], sems.at[0]),
        pltpu.make_async_copy(before, window.at[pl.ds(0, W)], sems.at[1]),
        pltpu.make_async_copy(nbr_hbm, nbr, sems.at[2]),
        pltpu.make_async_copy(cnt_hbm, cnt, sems.at[3]),
    ]
    for copy in copies:
        copy.start()
    run = all_rows(
        ((count, own0), (own2, rows)), count, 0, 0, nbr, cnt, table, blocks, window, applied, turned, items, row_sems, a_hbm, acc
    )
    skip = table[T_AGG + own0 + W] - AD
    resume = table[T_AGG + own2 + W] - AD
    clear(acc, HALF + 1, HALF + 1 + skip * KC)
    clear(acc, HALF + 1 + resume * KC, HALF + 1 + AD * KC)
    merge[T_N] = 0
    merge[T_H] = 0

    @pl.when(pos + 1 < devices)
    def _():
        begins = [table[T_NEXT + at] for at in range(4)]
        scan_rows(pos + 1, devices, rows, begins, merge)
        scan_sent(rows, begins, merge, True)

    split = merge[T_H]

    def add(slot, carry):
        acc[HALF + 1 + merge[T_DST + slot]] += got[slot - split].astype(jnp.float32)
        return carry

    lax.fori_loop(split, merge[T_N], add, 0)
    finish0 = write_own(last + 1, AD, acc, coarse, out_sems)
    for at in range(W):
        window[W + rows + at] = got[HALF + at]
    copies[2].wait()
    copies[3].wait()
    copies[0].wait()
    copies[1].wait()
    run()
    finish1 = write_own(0, skip, acc, coarse, out_sems)
    finish2 = write_own(resume, last + 1, acc, coarse, out_sems)
    merge[T_LAST] = last
    finish0()
    finish1()
    finish2()


def merge_kernel(merge, got, coarse, out, held, edge, sems, edge_sem):
    last = merge[T_LAST] * KC
    split = merge[T_H]
    copy = pltpu.make_async_copy(coarse.at[pl.ds(last, KC)], edge, edge_sem)
    copy.start()

    def store(slot):
        return pltpu.make_async_copy(held.at[slot], out.at[merge[T_DST + slot]], sems.at[slot])

    def alone(slot, carry):
        @pl.when(merge[T_DST + slot] >= last + KC)
        def _():
            held[slot] = got[slot].astype(jnp.float32)
            store(slot).start()

        return carry

    def shared(slot, carry):
        at = merge[T_DST + slot] - last

        @pl.when(at < KC)
        def _():
            held[slot] = got[slot].astype(jnp.float32) + edge[at]
            store(slot).start()

        return carry

    def wait(slot, carry):
        store(slot).wait()
        return carry

    lax.fori_loop(0, split, alone, 0)
    copy.wait()
    lax.fori_loop(0, split, shared, 0)
    lax.fori_loop(0, split, wait, 0)


SMEM = pl.BlockSpec(memory_space=pltpu.SMEM)
VMEM = pl.BlockSpec(memory_space=pltpu.VMEM)
HBM = pl.BlockSpec(memory_space=pltpu.HBM)
DMA = pltpu.SemaphoreType.DMA


def params(size=58):
    return pltpu.CompilerParams(vmem_limit_bytes=size * 1024 * 1024)


def cost(flops, moved):
    return pl.CostEstimate(flops=flops, bytes_accessed=moved, transcendentals=0)


def passed(block, step):
    devices = range(lax.axis_size(AXES))
    return lax.ppermute(block, AXES, [(i, i + step) for i in devices if i + step in devices])


def shards(a_blocks, nbr_offset, nbr_count, prolong, owner_start):
    devices = lax.axis_size(AXES)
    rows, slots, size, width = a_blocks.shape
    flops = rows * slots * size * size * width * 2
    moved = rows * slots * size * width * 2
    work = [
        pltpu.SMEM(nbr_offset.shape[::-1], jnp.int32),
        pltpu.SMEM(nbr_count.shape, jnp.int32),
        pltpu.VMEM((rows, slots, size, size), jnp.bfloat16),
        pltpu.VMEM((rows + 2 * W, size, width), jnp.bfloat16),
        [pltpu.VMEM((size, NQ * width), jnp.bfloat16)] * UNROLL,
        [pltpu.VMEM((width, size), jnp.bfloat16)] * UNROLL,
        pltpu.SMEM(((2 * W // NQ + 1) * (rows + 1),), jnp.int32),
        pltpu.VMEM((HALF + 1 + AD * KC, width, width), jnp.float32),
        DMA((4,)),
        DMA((rows,)),
        DMA((AD,)),
    ]
    table_shape = jax.ShapeDtypeStruct((T_LEN,), jnp.int32)
    coarse_shape = jax.ShapeDtypeStruct((AD * KC, width, width), jnp.float32)
    offsets = nbr_offset.T

    late, tail, coarse, table = pl.pallas_call(
        functools.partial(late_kernel, devices),
        out_shape=(
            jax.ShapeDtypeStruct((HALF + W, width, width), jnp.bfloat16),
            jax.ShapeDtypeStruct((W, size, width), jnp.bfloat16),
            coarse_shape,
            table_shape,
        ),
        in_specs=[HBM] * 5,
        out_specs=(VMEM, VMEM, HBM, SMEM),
        scratch_shapes=[pltpu.SMEM(owner_start.shape, jnp.int32)] + work,
        compiler_params=params(),
        cost_estimate=cost(flops // 3, moved // 3),
        name="late_rows",
    )(owner_start, offsets, nbr_count, a_blocks, prolong)
    before = passed(tail, 1)
    got_late = passed(late, -1)
    early, coarse = pl.pallas_call(
        functools.partial(early_kernel, devices),
        out_shape=(jax.ShapeDtypeStruct((HALF, width, width), jnp.bfloat16), coarse_shape),
        in_specs=[SMEM] + [HBM] * 6,
        out_specs=(VMEM, HBM),
        scratch_shapes=work,
        input_output_aliases={6: 1},
        compiler_params=params(),
        cost_estimate=cost(flops // 3, moved // 3),
        name="early_rows",
    )(table, offsets, nbr_count, a_blocks, prolong, before, coarse)
    got_early = passed(early, -1)
    coarse, merge = pl.pallas_call(
        functools.partial(own_kernel, devices),
        out_shape=(coarse_shape, table_shape),
        in_specs=[SMEM] + [HBM] * 5 + [VMEM, HBM],
        out_specs=(HBM, SMEM),
        scratch_shapes=work,
        input_output_aliases={7: 0},
        compiler_params=params(),
        cost_estimate=cost(flops // 3, moved // 3),
        name="own_rows",
    )(table, offsets, nbr_count, a_blocks, prolong, before, got_late, coarse)
    coarse = pl.pallas_call(
        merge_kernel,
        out_shape=coarse_shape,
        in_specs=[SMEM, VMEM, HBM],
        out_specs=HBM,
        scratch_shapes=[
            pltpu.VMEM((HALF, width, width), jnp.float32),
            pltpu.VMEM((KC, width, width), jnp.float32),
            DMA((HALF,)),
            DMA,
        ],
        input_output_aliases={2: 0},
        compiler_params=params(32),
        name="merge_rows",
    )(merge, got_early, coarse)
    return coarse.reshape(AD, KC, width, width)


def solution(mesh):
    placed = (
        P(("dom", "sub"), None, None, None),
        P(("dom", "sub"), None),
        P(("dom", "sub")),
        P(("dom", "sub"), None, None),
        P(),
    )
    return jax.shard_map(
        shards,
        mesh=mesh,
        in_specs=placed,
        out_specs=P(("dom", "sub"), None, None, None),
        check_vma=False,
    )
```

```python
import functools

import jax
import jax.numpy as jnp
from jax import lax
from jax.experimental import pallas as pl
from jax.experimental.pallas import tpu as pltpu
from jax.sharding import PartitionSpec as P

W = 3
KC = 7
AD = 16
SMAX = 48
NQ = 2
UNROLL = 6
HALF = 22
AXES = ("dom", "sub")


AHEAD = 16
SHIFT = 20
FAR = 1024

T_AGG = 0
T_OFF = 128
T_BASE = 192
T_ROW = 256
T_DST = 384
T_CUM = 512
T_COLUMN = 640
T_N = 448
T_H = 449
T_LO = 450
T_HI = 451
T_S = 452
T_OWN0 = 453
T_OWN1 = 454
T_OWN2 = 455
T_LAST = 456
T_NEXT = 457
T_GROUP = 128
T_LEN = 768


def starts(pos, devices, rows, own_ref):
    def start(owner):
        at = jnp.clip(owner, 0, devices - 1)
        given = jnp.where(owner < devices, own_ref[at], devices * rows)
        return jnp.where(owner < 0, 0, given) - pos * rows

    return [start(pos + step) for step in (-1, 0, 1, 2)]


def row_start(begin, length, agg):
    return begin + lax.shift_right_logical(agg * length + (AD - 1), 4)


def scan_rows(pos, devices, rows, begins, table):
    total = devices * rows
    first = pos * rows
    scale = []
    for owner in range(3):
        length = jnp.maximum(begins[owner + 1] - begins[owner], 1)
        scale.append(lax.div(length + (2**SHIFT - 1), length) * AD)
    items = jnp.int32(0)
    aggs = []
    for at in range(rows + 2 * W):
        row = at - W

        def local(owner):
            return lax.shift_right_logical((row - begins[owner]) * scale[owner], SHIFT) + owner * AD

        if row >= rows:
            agg = jnp.where(row >= begins[2], local(2), local(1))
            agg = jnp.where(first + row < total, agg, aggs[-1])
            column = jnp.where(first + row < total, agg, FAR)
        elif row >= SMAX:
            agg = column = local(1)
        elif row >= 0:
            agg = column = jnp.where(row >= begins[1], local(1), local(0))
        else:
            agg = jnp.where(first > 0, local(0), AD)
            column = jnp.where(first > 0, agg, FAR)
        aggs.append(agg)
        table[T_AGG + at] = agg
        table[T_COLUMN + at] = column
        if at >= 2 * W:
            table[T_CUM + at - 2 * W] = items
            items = items + (lax.shift_right_logical(agg - aggs[at - 2 * W], 1) + 1)
    table[T_CUM + rows] = items


def scan_sent(rows, begins, table, places):
    count = begins[1]
    length = begins[1] - begins[0]
    sent = table[T_CUM + count]
    share = jnp.maximum(lax.div(table[T_CUM + rows], 3), lax.div(7 * sent, 16))
    lowest = jnp.where(count > 0, table[T_AGG + W], AD)

    def span(agg):
        return (
            jnp.maximum(row_start(begins[0], length, agg), 0),
            jnp.minimum(row_start(begins[0], length, agg + 1), count),
        )

    def step(agg, carry):
        end, floor, even = carry
        row, stop = span(agg)
        off = end - table[T_AGG + row]
        table[T_OFF + agg] = off
        table[T_BASE + agg] = end
        table[T_ROW + agg] = row
        begin = end
        end = off + table[T_AGG + stop - 1 + 2 * W] + 1
        if places:

            def put(slot, carry):
                table[T_DST + slot] = (KC - 1) * agg + W + slot - off
                return carry

            lax.fori_loop(begin, end, put, 0)
        floor = jnp.where(row < W, end, floor)
        even = jnp.where(sent - table[T_CUM + row] > share, end, even)
        return end, floor, even

    end, floor, even = lax.fori_loop(lowest, AD, step, (0, 0, 0))
    split = jnp.maximum(jnp.maximum(end - HALF, floor), jnp.minimum(even, HALF))
    table[T_N] = end
    table[T_H] = split
    if places:
        return

    def find(agg, carry):
        low, high = carry
        base = table[T_BASE + agg]
        row, stop = span(agg)
        low = jnp.where(base <= split, row, low)
        high = jnp.where(base < split, stop, high)
        return low, high

    low, high = lax.fori_loop(lowest, AD, find, (0, 0))
    table[T_LO] = jnp.where(split >= end, count, low)
    table[T_HI] = high


def share_own(rows, begins, table):
    count = begins[1]
    length = begins[2] - begins[1]
    whole = table[T_CUM + rows]
    first = jnp.maximum(lax.div(whole, 3) - table[T_CUM + count] + table[T_CUM + table[T_LO]], 0)
    second = jnp.maximum(lax.div(3 * whole, 8) - table[T_CUM + table[T_HI]], 0)

    def step(agg, carry):
        own0, own1, own2 = carry
        row = row_start(count, length, agg)
        fresh = (row >= W) & (own0 < 0)
        own0 = jnp.where(fresh, row, own0)
        own1 = jnp.where(fresh, row, own1)
        own2 = jnp.where(fresh, row, own2)
        inside = (own0 >= 0) & (row <= rows - W)
        done = table[T_CUM + row]
        own1 = jnp.where(inside & (done <= table[T_CUM + jnp.maximum(own0, 0)] + first), row, own1)
        own2 = jnp.where(inside & (done <= table[T_CUM + jnp.maximum(own1, 0)] + second), row, own2)
        return own0, own1, own2

    own0, own1, own2 = lax.fori_loop(0, AD, step, (-1, -1, -1))
    table[T_OWN0] = own0
    table[T_OWN1] = own1
    table[T_OWN2] = own2
    table[T_S] = count
    table[T_LAST] = table[T_AGG + rows - 1 + W] - AD


def apply_row(row, group, nbr, cnt, table, blocks, window, applied):
    right = []
    left = []
    slots = cnt[row]
    lowest = table[T_AGG + row] + NQ * group
    for k in range(blocks.shape[1]):
        at = row + W + nbr[k, row]
        near = window[at]
        column = jnp.where(k < slots, table[T_COLUMN + at], FAR) - lowest
        zero = jnp.zeros_like(near)
        right.append(jnp.concatenate([jnp.where(column == q, near, zero) for q in range(NQ)], axis=1))
        left.append(blocks[row, k])
    applied[...] = jnp.dot(
        jnp.concatenate(left, axis=1), jnp.concatenate(right, axis=0), preferred_element_type=jnp.float32
    ).astype(applied.dtype)


def all_rows(ranges, down, ahead, low_slot, high_slot, nbr, cnt, table, blocks, window, applied, turned, items, row_sems, a_hbm, acc):
    (lo0, hi0), (lo1, hi1) = ranges
    width = window.shape[2]
    count = table[T_S]
    turn = hi0 - lo0

    def row_at(index):
        sent = hi0 - 1 - index if down else lo0 + index
        return jnp.where(index < turn, sent, lo1 + index - turn)

    def start(index, amount):
        row = row_at(index)

        @pl.when((row < ahead) | (row >= count))
        def _():
            pltpu.make_async_copy(a_hbm.at[row], blocks.at[row], row_sems.at[row]).start()

        for group in range((2 * W) // NQ + 1):
            items[amount + group] = row + T_GROUP * group
        return amount + table[T_CUM + row + 1] - table[T_CUM + row]

    amount = lax.fori_loop(0, turn + hi1 - lo1, start, 0)

    def item(index):
        at = items[jnp.clip(index, 0, amount - 1)]
        valid = (index >= 0) & (index < amount)
        return at & (T_GROUP - 1), lax.shift_right_logical(at, 7), valid

    def add(row, group, valid, u):
        term = jnp.dot(turned[u][...], applied[u][...], preferred_element_type=jnp.float32)
        agg = table[T_AGG + row + W]
        highest = table[T_AGG + row + 2 * W]
        own = row >= count
        for q in range(NQ):
            target = table[T_AGG + row] + NQ * group + q
            sent = table[T_OFF + agg] + target
            kept = (KC - 1) * agg - KC * AD + W + target
            ok = valid & (target <= highest) & (own | ((sent >= low_slot) & (sent < high_slot)))
            at = jnp.where(ok, jnp.where(own, HALF + 1 + kept, sent - low_slot), HALF)
            acc[at] += term[:, q * width : (q + 1) * width]

    def add_block(begin):
        for u in range(UNROLL):
            row, group, valid = item(begin + u)
            add(row, group, valid, u)

    def block(step, carry):
        begin = step * UNROLL
        for u in range(UNROLL):
            row, group, valid = item(begin + u)

            @pl.when(valid & (group == 0))
            def _():
                pltpu.make_async_copy(a_hbm.at[row], blocks.at[row], row_sems.at[row]).wait()

        add_block(begin - UNROLL)
        for u in range(UNROLL):
            row, group, valid = item(begin + u)
            apply_row(row, group, nbr, cnt, table, blocks, window, applied[u])
            turned[u][...] = window[row + W].T
        return carry

    def run():
        @pl.when(amount > 0)
        def _():
            steps = lax.div(amount + UNROLL - 1, UNROLL)
            lax.fori_loop(0, steps, block, 0)
            add_block((steps - 1) * UNROLL)

    return run


def clear(acc, begin, end):
    def step(at, carry):
        acc[at] = jnp.zeros(acc.shape[1:], acc.dtype)
        return carry

    lax.fori_loop(begin, end, step, 0)


def give(acc, out):
    def step(at, carry):
        out[at] = acc[at].astype(out.dtype)
        return carry

    lax.fori_loop(0, HALF, step, 0)


def write_own(begin, end, acc, coarse, sems):
    def copy(agg):
        return pltpu.make_async_copy(
            acc.at[pl.ds(HALF + 1 + agg * KC, KC)], coarse.at[pl.ds(agg * KC, KC)], sems.at[agg]
        )

    def start(agg, carry):
        copy(agg).start()
        return carry

    def wait(agg, carry):
        copy(agg).wait()
        return carry

    lax.fori_loop(begin, end, start, 0)
    return lambda: lax.fori_loop(begin, end, wait, 0)


def position():
    place = 0
    for axis in AXES:
        place = place * lax.axis_size(axis) + lax.axis_index(axis)
    return place


def late_kernel(
    devices, own_hbm, nbr_hbm, cnt_hbm, a_hbm, p_hbm, out, tail, coarse, table, own, nbr, cnt, blocks, window, applied, turned, items, acc, sems, row_sems, out_sems
):
    rows = a_hbm.shape[0]
    pos = position()
    copies = [
        pltpu.make_async_copy(own_hbm, own, sems.at[0]),
        pltpu.make_async_copy(nbr_hbm, nbr, sems.at[1]),
        pltpu.make_async_copy(cnt_hbm, cnt, sems.at[2]),
        pltpu.make_async_copy(p_hbm, window.at[pl.ds(W, rows)], sems.at[3]),
    ]
    for copy in copies:
        copy.start()
    copies[0].wait()
    begins = starts(pos, devices, rows, own)
    for at, begin in enumerate(starts(pos + 1, devices, rows, own)):
        table[T_NEXT + at] = begin
    count = begins[1]
    ahead = jnp.maximum(count - AHEAD, W)

    def fetch(row):
        return pltpu.make_async_copy(a_hbm.at[row], blocks.at[row], row_sems.at[row])

    def prefetch(index, carry):
        fetch(count - 1 - index).start()
        return carry

    def drain(row, carry):
        fetch(row).wait()
        return carry

    lax.fori_loop(0, count - ahead, prefetch, 0)
    scan_rows(pos, devices, rows, begins, table)
    scan_sent(rows, begins, table, False)
    share_own(rows, begins, table)
    low, own0, own1 = table[T_LO], table[T_OWN0], table[T_OWN1]
    run = all_rows(
        ((low, count), (own0, own1)), True, ahead, table[T_H], table[T_N], nbr, cnt, table, blocks, window, applied, turned, items, row_sems, a_hbm, acc
    )
    begin = table[T_AGG + own0 + W] - AD
    stop = table[T_AGG + own1 + W] - AD
    clear(acc, 0, HALF)
    clear(acc, HALF + 1 + begin * KC, HALF + 1 + stop * KC)
    copies[1].wait()
    copies[2].wait()
    copies[3].wait()
    for at in range(W):
        out[HALF + at] = window[W + at]
        tail[at] = window[rows + at]
    run()
    finish = write_own(begin, stop, acc, coarse, out_sems)
    give(acc, out)
    lax.fori_loop(ahead, low, drain, 0)
    finish()


def early_kernel(
    devices, table, nbr_hbm, cnt_hbm, a_hbm, p_hbm, before, _, out, coarse, nbr, cnt, blocks, window, applied, turned, items, acc, sems, row_sems, out_sems
):
    rows = a_hbm.shape[0]
    pos = position()
    own1, own2 = table[T_OWN1], table[T_OWN2]
    copies = [
        pltpu.make_async_copy(p_hbm, window.at[pl.ds(W, rows)], sems.at[0]),
        pltpu.make_async_copy(before, window.at[pl.ds(0, W)], sems.at[1]),
        pltpu.make_async_copy(nbr_hbm, nbr, sems.at[2]),
        pltpu.make_async_copy(cnt_hbm, cnt, sems.at[3]),
    ]
    for copy in copies:
        copy.start()
    run = all_rows(
        ((0, table[T_HI]), (own1, own2)), False, table[T_S], 0, table[T_H], nbr, cnt, table, blocks, window, applied, turned, items, row_sems, a_hbm, acc
    )
    begin = table[T_AGG + own1 + W] - AD
    stop = table[T_AGG + own2 + W] - AD
    clear(acc, 0, HALF)
    clear(acc, HALF + 1 + begin * KC, HALF + 1 + stop * KC)
    copies[2].wait()
    copies[3].wait()
    copies[0].wait()
    copies[1].wait()
    run()
    finish = write_own(begin, stop, acc, coarse, out_sems)
    give(acc, out)
    finish()


def own_kernel(
    devices, table, nbr_hbm, cnt_hbm, a_hbm, p_hbm, before, got, _, coarse, edge, merge, nbr, cnt, blocks, window, applied, turned, items, acc, sems, row_sems, out_sems
):
    rows = a_hbm.shape[0]
    pos = position()
    count, own0, own2, last = table[T_S], table[T_OWN0], table[T_OWN2], table[T_LAST]
    copies = [
        pltpu.make_async_copy(p_hbm, window.at[pl.ds(W, rows)], sems.at[0]),
        pltpu.make_async_copy(before, window.at[pl.ds(0, W)], sems.at[1]),
        pltpu.make_async_copy(nbr_hbm, nbr, sems.at[2]),
        pltpu.make_async_copy(cnt_hbm, cnt, sems.at[3]),
    ]
    for copy in copies:
        copy.start()
    run = all_rows(
        ((count, own0), (own2, rows)), False, count, 0, 0, nbr, cnt, table, blocks, window, applied, turned, items, row_sems, a_hbm, acc
    )
    skip = table[T_AGG + own0 + W] - AD
    resume = table[T_AGG + own2 + W] - AD
    clear(acc, HALF + 1, HALF + 1 + skip * KC)
    clear(acc, HALF + 1 + resume * KC, HALF + 1 + AD * KC)
    merge[T_N] = 0
    merge[T_H] = 0

    @pl.when(pos + 1 < devices)
    def _():
        begins = [table[T_NEXT + at] for at in range(4)]
        scan_rows(pos + 1, devices, rows, begins, merge)
        scan_sent(rows, begins, merge, True)

    split = merge[T_H]

    def add(slot, carry):
        acc[HALF + 1 + merge[T_DST + slot]] += got[slot - split].astype(jnp.float32)
        return carry

    lax.fori_loop(split, merge[T_N], add, 0)
    finish0 = write_own(last + 1, AD, acc, coarse, out_sems)
    for at in range(W):
        window[W + rows + at] = got[HALF + at]
    copies[2].wait()
    copies[3].wait()
    copies[0].wait()
    copies[1].wait()
    run()
    finish1 = write_own(0, skip, acc, coarse, out_sems)
    finish2 = write_own(resume, last + 1, acc, coarse, out_sems)
    for at in range(KC):
        edge[at] = acc[HALF + 1 + last * KC + at]
    merge[T_LAST] = last
    finish0()
    finish1()
    finish2()


def merge_kernel(merge, got, edge, _, coarse, held, sems):
    last = merge[T_LAST] * KC

    def store(slot):
        return pltpu.make_async_copy(held.at[slot], coarse.at[merge[T_DST + slot]], sems.at[slot])

    def start(slot, carry):
        at = merge[T_DST + slot] - last
        base = edge[jnp.minimum(at, KC - 1)]
        held[slot] = got[slot].astype(jnp.float32) + jnp.where(at < KC, base, jnp.zeros_like(base))
        store(slot).start()
        return carry

    def wait(slot, carry):
        store(slot).wait()
        return carry

    lax.fori_loop(0, merge[T_H], start, 0)
    lax.fori_loop(0, merge[T_H], wait, 0)


SMEM = pl.BlockSpec(memory_space=pltpu.SMEM)
VMEM = pl.BlockSpec(memory_space=pltpu.VMEM)
HBM = pl.BlockSpec(memory_space=pltpu.HBM)
DMA = pltpu.SemaphoreType.DMA


def params(size=58):
    return pltpu.CompilerParams(vmem_limit_bytes=size * 1024 * 1024)


def cost(flops, moved):
    return pl.CostEstimate(flops=flops, bytes_accessed=moved, transcendentals=0)


def passed(block, step):
    devices = range(lax.axis_size(AXES))
    return lax.ppermute(block, AXES, [(i, i + step) for i in devices if i + step in devices])


def shards(a_blocks, nbr_offset, nbr_count, prolong, owner_start):
    devices = lax.axis_size(AXES)
    rows, slots, size, width = a_blocks.shape
    flops = rows * slots * size * size * width * 2
    moved = rows * slots * size * width * 2
    work = [
        pltpu.SMEM(nbr_offset.shape[::-1], jnp.int32),
        pltpu.SMEM(nbr_count.shape, jnp.int32),
        pltpu.VMEM((rows, slots, size, size), jnp.bfloat16),
        pltpu.VMEM((rows + 2 * W, size, width), jnp.bfloat16),
        [pltpu.VMEM((size, NQ * width), jnp.bfloat16)] * UNROLL,
        [pltpu.VMEM((width, size), jnp.bfloat16)] * UNROLL,
        pltpu.SMEM(((2 * W // NQ + 1) * (rows + 1),), jnp.int32),
        pltpu.VMEM((HALF + 1 + AD * KC, width, width), jnp.float32),
        DMA((4,)),
        DMA((rows,)),
        DMA((AD,)),
    ]
    table_shape = jax.ShapeDtypeStruct((T_LEN,), jnp.int32)
    coarse_shape = jax.ShapeDtypeStruct((AD * KC, width, width), jnp.float32)
    offsets = nbr_offset.T

    late, tail, coarse, table = pl.pallas_call(
        functools.partial(late_kernel, devices),
        out_shape=(
            jax.ShapeDtypeStruct((HALF + W, width, width), jnp.bfloat16),
            jax.ShapeDtypeStruct((W, size, width), jnp.bfloat16),
            coarse_shape,
            table_shape,
        ),
        in_specs=[HBM] * 5,
        out_specs=(VMEM, VMEM, HBM, SMEM),
        scratch_shapes=[pltpu.SMEM(owner_start.shape, jnp.int32)] + work,
        compiler_params=params(),
        cost_estimate=cost(flops // 3, moved // 3),
        name="late_rows",
    )(owner_start, offsets, nbr_count, a_blocks, prolong)
    before = passed(tail, 1)
    got_late = passed(late, -1)
    early, coarse = pl.pallas_call(
        functools.partial(early_kernel, devices),
        out_shape=(jax.ShapeDtypeStruct((HALF, width, width), jnp.bfloat16), coarse_shape),
        in_specs=[SMEM] + [HBM] * 6,
        out_specs=(VMEM, HBM),
        scratch_shapes=work,
        input_output_aliases={6: 1},
        compiler_params=params(50),
        cost_estimate=cost(flops // 3, moved // 3),
        name="early_rows",
    )(table, offsets, nbr_count, a_blocks, prolong, before, coarse)
    got_early = passed(early, -1)
    coarse, edge, merge = pl.pallas_call(
        functools.partial(own_kernel, devices),
        out_shape=(coarse_shape, jax.ShapeDtypeStruct((KC, width, width), jnp.float32), table_shape),
        in_specs=[SMEM] + [HBM] * 5 + [VMEM, HBM],
        out_specs=(HBM, VMEM, SMEM),
        scratch_shapes=work,
        input_output_aliases={7: 0},
        compiler_params=params(50),
        cost_estimate=cost(flops // 3, moved // 3),
        name="own_rows",
    )(table, offsets, nbr_count, a_blocks, prolong, before, got_late, coarse)
    coarse = pl.pallas_call(
        merge_kernel,
        out_shape=coarse_shape,
        in_specs=[SMEM, VMEM, VMEM, HBM],
        out_specs=HBM,
        scratch_shapes=[pltpu.VMEM((HALF, width, width), jnp.float32), DMA((HALF,))],
        input_output_aliases={3: 0},
        compiler_params=params(32),
        name="merge_rows",
    )(merge, got_early, edge, coarse)
    return coarse.reshape(AD, KC, width, width)


def solution(mesh):
    placed = (
        P(("dom", "sub"), None, None, None),
        P(("dom", "sub"), None),
        P(("dom", "sub")),
        P(("dom", "sub"), None, None),
        P(),
    )
    return jax.shard_map(
        shards,
        mesh=mesh,
        in_specs=placed,
        out_specs=P(("dom", "sub"), None, None, None),
        check_vma=False,
    )
```

```python
import functools

import jax
import jax.numpy as jnp
from jax import lax
from jax.experimental import pallas as pl
from jax.experimental.pallas import tpu as pltpu
from jax.sharding import PartitionSpec as P

W = 3
KC = 7
AD = 16
SMAX = 48
NQ = 2
UNROLL = 6
HALF = 22
AXES = ("dom", "sub")


AHEAD = 16
SHIFT = 20
FAR = 1024

T_AGG = 0
T_OFF = 128
T_BASE = 192
T_ROW = 256
T_DST = 384
T_CUM = 512
T_COLUMN = 640
T_N = 448
T_H = 449
T_LO = 450
T_HI = 451
T_S = 452
T_OWN0 = 453
T_OWN1 = 454
T_OWN2 = 455
T_LAST = 456
T_NEXT = 457
T_GROUP = 128
T_LEN = 768


def starts(pos, devices, rows, own_ref):
    def start(owner):
        at = jnp.clip(owner, 0, devices - 1)
        given = jnp.where(owner < devices, own_ref[at], devices * rows)
        return jnp.where(owner < 0, 0, given) - pos * rows

    return [start(pos + step) for step in (-1, 0, 1, 2)]


def row_start(begin, length, agg):
    return begin + lax.shift_right_logical(agg * length + (AD - 1), 4)


def scan_rows(pos, devices, rows, begins, table):
    total = devices * rows
    first = pos * rows
    scale = []
    for owner in range(3):
        length = jnp.maximum(begins[owner + 1] - begins[owner], 1)
        scale.append(lax.div(length + (2**SHIFT - 1), length) * AD)
    items = jnp.int32(0)
    aggs = []
    for at in range(rows + 2 * W):
        row = at - W

        def local(owner):
            return lax.shift_right_logical((row - begins[owner]) * scale[owner], SHIFT) + owner * AD

        if row >= rows:
            agg = jnp.where(row >= begins[2], local(2), local(1))
            agg = jnp.where(first + row < total, agg, aggs[-1])
            column = jnp.where(first + row < total, agg, FAR)
        elif row >= SMAX:
            agg = column = local(1)
        elif row >= 0:
            agg = column = jnp.where(row >= begins[1], local(1), local(0))
        else:
            agg = jnp.where(first > 0, local(0), AD)
            column = jnp.where(first > 0, agg, FAR)
        aggs.append(agg)
        table[T_AGG + at] = agg
        table[T_COLUMN + at] = column
        if at >= 2 * W:
            table[T_CUM + at - 2 * W] = items
            items = items + (lax.shift_right_logical(agg - aggs[at - 2 * W], 1) + 1)
    table[T_CUM + rows] = items


def scan_sent(rows, begins, table, places):
    count = begins[1]
    length = begins[1] - begins[0]
    sent = table[T_CUM + count]
    share = jnp.maximum(lax.div(table[T_CUM + rows], 3), lax.div(7 * sent, 16))
    lowest = jnp.where(count > 0, table[T_AGG + W], AD)

    def span(agg):
        return (
            jnp.maximum(row_start(begins[0], length, agg), 0),
            jnp.minimum(row_start(begins[0], length, agg + 1), count),
        )

    def step(agg, carry):
        end, floor, even = carry
        row, stop = span(agg)
        off = end - table[T_AGG + row]
        table[T_OFF + agg] = off
        table[T_BASE + agg] = end
        table[T_ROW + agg] = row
        begin = end
        end = off + table[T_AGG + stop - 1 + 2 * W] + 1
        if places:

            def put(slot, carry):
                table[T_DST + slot] = (KC - 1) * agg + W + slot - off
                return carry

            lax.fori_loop(begin, end, put, 0)
        floor = jnp.where(row < W, end, floor)
        even = jnp.where(sent - table[T_CUM + row] > share, end, even)
        return end, floor, even

    end, floor, even = lax.fori_loop(lowest, AD, step, (0, 0, 0))
    split = jnp.maximum(jnp.maximum(end - HALF, floor), jnp.minimum(even, HALF))
    table[T_N] = end
    table[T_H] = split
    if places:
        return

    def find(agg, carry):
        low, high = carry
        base = table[T_BASE + agg]
        row, stop = span(agg)
        low = jnp.where(base <= split, row, low)
        high = jnp.where(base < split, stop, high)
        return low, high

    low, high = lax.fori_loop(lowest, AD, find, (0, 0))
    table[T_LO] = jnp.where(split >= end, count, low)
    table[T_HI] = high


def share_own(rows, begins, table):
    count = begins[1]
    length = begins[2] - begins[1]
    whole = table[T_CUM + rows]
    first = jnp.maximum(lax.div(whole, 3) - table[T_CUM + count] + table[T_CUM + table[T_LO]], 0)
    second = jnp.maximum(lax.div(3 * whole, 8) - table[T_CUM + table[T_HI]], 0)

    def step(agg, carry):
        own0, own1, own2 = carry
        row = row_start(count, length, agg)
        fresh = (row >= W) & (own0 < 0)
        own0 = jnp.where(fresh, row, own0)
        own1 = jnp.where(fresh, row, own1)
        own2 = jnp.where(fresh, row, own2)
        inside = (own0 >= 0) & (row <= rows - W)
        done = table[T_CUM + row]
        own1 = jnp.where(inside & (done <= table[T_CUM + jnp.maximum(own0, 0)] + first), row, own1)
        own2 = jnp.where(inside & (done <= table[T_CUM + jnp.maximum(own1, 0)] + second), row, own2)
        return own0, own1, own2

    own0, own1, own2 = lax.fori_loop(0, AD, step, (-1, -1, -1))
    table[T_OWN0] = own0
    table[T_OWN1] = own1
    table[T_OWN2] = own2
    table[T_S] = count
    table[T_LAST] = table[T_AGG + rows - 1 + W] - AD


def apply_row(row, group, nbr, cnt, table, blocks, window, applied):
    right = []
    left = []
    slots = cnt[row]
    lowest = table[T_AGG + row] + NQ * group
    for k in range(blocks.shape[1]):
        at = row + W + nbr[k, row]
        near = window[at]
        column = jnp.where(k < slots, table[T_COLUMN + at], FAR) - lowest
        zero = jnp.zeros_like(near)
        right.append(jnp.concatenate([jnp.where(column == q, near, zero) for q in range(NQ)], axis=1))
        left.append(blocks[row, k])
    applied[...] = jnp.dot(
        jnp.concatenate(left, axis=1), jnp.concatenate(right, axis=0), preferred_element_type=jnp.float32
    ).astype(applied.dtype)


def all_rows(ranges, down, ahead, low_slot, high_slot, nbr, cnt, table, blocks, window, applied, turned, items, row_sems, a_hbm, acc, writes):
    (lo0, hi0), (lo1, hi1) = ranges
    width = window.shape[2]
    count = table[T_S]
    turn = hi0 - lo0

    def row_at(index):
        sent = hi0 - 1 - index if down else lo0 + index
        return jnp.where(index < turn, sent, lo1 + index - turn)

    def start(index, amount):
        row = row_at(index)

        @pl.when((row < ahead) | (row >= count))
        def _():
            pltpu.make_async_copy(a_hbm.at[row], blocks.at[row], row_sems.at[row]).start()

        for group in range((2 * W) // NQ + 1):
            items[amount + group] = row + T_GROUP * group
        return amount + table[T_CUM + row + 1] - table[T_CUM + row]

    amount = lax.fori_loop(0, turn + hi1 - lo1, start, 0)

    def item(index):
        at = items[jnp.clip(index, 0, amount - 1)]
        valid = (index >= 0) & (index < amount)
        return at & (T_GROUP - 1), lax.shift_right_logical(at, 7), valid

    def add(row, group, valid, u):
        term = jnp.dot(turned[u][...], applied[u][...], preferred_element_type=jnp.float32)
        agg = table[T_AGG + row + W]
        highest = table[T_AGG + row + 2 * W]
        own = row >= count
        for q in range(NQ):
            target = table[T_AGG + row] + NQ * group + q
            sent = table[T_OFF + agg] + target
            kept = (KC - 1) * agg - KC * AD + W + target
            ok = valid & (target <= highest) & (own | ((sent >= low_slot) & (sent < high_slot)))
            at = jnp.where(ok, jnp.where(own, HALF + 1 + kept, sent - low_slot), HALF)
            acc[at] += term[:, q * width : (q + 1) * width]

    def add_block(begin):
        for u in range(UNROLL):
            row, group, valid = item(begin + u)
            add(row, group, valid, u)

    def block(step, written):
        begin = step * UNROLL
        row, _, valid = item(begin - UNROLL)
        whole = jnp.where(valid, jnp.clip(table[T_AGG + row + W] - AD, 0, AD), 0)
        writes.start(written, whole)
        for u in range(UNROLL):
            row, group, valid = item(begin + u)

            @pl.when(valid & (group == 0))
            def _():
                pltpu.make_async_copy(a_hbm.at[row], blocks.at[row], row_sems.at[row]).wait()

        add_block(begin - UNROLL)
        for u in range(UNROLL):
            row, group, valid = item(begin + u)
            apply_row(row, group, nbr, cnt, table, blocks, window, applied[u])
            turned[u][...] = window[row + W].T
        return jnp.maximum(written, whole)

    def run():
        @pl.when(amount > 0)
        def _():
            steps = lax.div(amount + UNROLL - 1, UNROLL)
            written = lax.fori_loop(0, steps, block, jnp.int32(0))
            add_block((steps - 1) * UNROLL)
            writes.start(written, AD)

    return run


def clear(acc, begin, end):
    def step(at, carry):
        acc[at] = jnp.zeros(acc.shape[1:], acc.dtype)
        return carry

    lax.fori_loop(begin, end, step, 0)


def give(acc, out):
    def step(at, carry):
        out[at] = acc[at].astype(out.dtype)
        return carry

    lax.fori_loop(0, HALF, step, 0)


class Writes:
    def __init__(self, ranges, acc, coarse, sems):
        self.ranges, self.acc, self.coarse, self.sems = ranges, acc, coarse, sems

    def each(self, begin, end, act):
        def step(agg, carry):
            inside = False
            for low, high in self.ranges:
                inside = inside | ((agg >= low) & (agg < high))

            @pl.when(inside)
            def _():
                act(
                    pltpu.make_async_copy(
                        self.acc.at[pl.ds(HALF + 1 + agg * KC, KC)],
                        self.coarse.at[pl.ds(agg * KC, KC)],
                        self.sems.at[agg],
                    )
                )

            return carry

        lax.fori_loop(begin, end, step, 0)

    def start(self, begin, end):
        self.each(begin, end, lambda copy: copy.start())

    def wait(self):
        self.each(0, AD, lambda copy: copy.wait())


def position():
    place = 0
    for axis in AXES:
        place = place * lax.axis_size(axis) + lax.axis_index(axis)
    return place


def late_kernel(
    devices, own_hbm, nbr_hbm, cnt_hbm, a_hbm, p_hbm, out, tail, coarse, table, own, nbr, cnt, blocks, window, applied, turned, items, acc, sems, row_sems, out_sems
):
    rows = a_hbm.shape[0]
    pos = position()
    copies = [
        pltpu.make_async_copy(own_hbm, own, sems.at[0]),
        pltpu.make_async_copy(nbr_hbm, nbr, sems.at[1]),
        pltpu.make_async_copy(cnt_hbm, cnt, sems.at[2]),
        pltpu.make_async_copy(p_hbm, window.at[pl.ds(W, rows)], sems.at[3]),
    ]
    for copy in copies:
        copy.start()
    copies[0].wait()
    begins = starts(pos, devices, rows, own)
    for at, begin in enumerate(starts(pos + 1, devices, rows, own)):
        table[T_NEXT + at] = begin
    count = begins[1]
    ahead = jnp.maximum(count - AHEAD, W)

    def fetch(row):
        return pltpu.make_async_copy(a_hbm.at[row], blocks.at[row], row_sems.at[row])

    def prefetch(index, carry):
        fetch(count - 1 - index).start()
        return carry

    def drain(row, carry):
        fetch(row).wait()
        return carry

    lax.fori_loop(0, count - ahead, prefetch, 0)
    scan_rows(pos, devices, rows, begins, table)
    scan_sent(rows, begins, table, False)
    share_own(rows, begins, table)
    low, own0, own1 = table[T_LO], table[T_OWN0], table[T_OWN1]
    begin = table[T_AGG + own0 + W] - AD
    stop = table[T_AGG + own1 + W] - AD
    writes = Writes([(begin, stop)], acc, coarse, out_sems)
    run = all_rows(
        ((low, count), (own0, own1)), True, ahead, table[T_H], table[T_N], nbr, cnt, table, blocks, window, applied, turned, items, row_sems, a_hbm, acc, writes
    )
    clear(acc, 0, HALF)
    clear(acc, HALF + 1 + begin * KC, HALF + 1 + stop * KC)
    copies[1].wait()
    copies[2].wait()
    copies[3].wait()
    for at in range(W):
        out[HALF + at] = window[W + at]
        tail[at] = window[rows + at]
    run()
    give(acc, out)
    lax.fori_loop(ahead, low, drain, 0)
    writes.wait()


def early_kernel(
    devices, table, nbr_hbm, cnt_hbm, a_hbm, p_hbm, before, _, out, coarse, nbr, cnt, blocks, window, applied, turned, items, acc, sems, row_sems, out_sems
):
    rows = a_hbm.shape[0]
    pos = position()
    own1, own2 = table[T_OWN1], table[T_OWN2]
    copies = [
        pltpu.make_async_copy(p_hbm, window.at[pl.ds(W, rows)], sems.at[0]),
        pltpu.make_async_copy(before, window.at[pl.ds(0, W)], sems.at[1]),
        pltpu.make_async_copy(nbr_hbm, nbr, sems.at[2]),
        pltpu.make_async_copy(cnt_hbm, cnt, sems.at[3]),
    ]
    for copy in copies:
        copy.start()
    begin = table[T_AGG + own1 + W] - AD
    stop = table[T_AGG + own2 + W] - AD
    writes = Writes([(begin, stop)], acc, coarse, out_sems)
    run = all_rows(
        ((0, table[T_HI]), (own1, own2)), False, table[T_S], 0, table[T_H], nbr, cnt, table, blocks, window, applied, turned, items, row_sems, a_hbm, acc, writes
    )
    clear(acc, 0, HALF)
    clear(acc, HALF + 1 + begin * KC, HALF + 1 + stop * KC)
    copies[2].wait()
    copies[3].wait()
    copies[0].wait()
    copies[1].wait()
    run()
    give(acc, out)
    writes.wait()


def own_kernel(
    devices, table, nbr_hbm, cnt_hbm, a_hbm, p_hbm, before, got, _, coarse, edge, merge, nbr, cnt, blocks, window, applied, turned, items, acc, sems, row_sems, out_sems
):
    rows = a_hbm.shape[0]
    pos = position()
    count, own0, own2, last = table[T_S], table[T_OWN0], table[T_OWN2], table[T_LAST]
    copies = [
        pltpu.make_async_copy(p_hbm, window.at[pl.ds(W, rows)], sems.at[0]),
        pltpu.make_async_copy(before, window.at[pl.ds(0, W)], sems.at[1]),
        pltpu.make_async_copy(nbr_hbm, nbr, sems.at[2]),
        pltpu.make_async_copy(cnt_hbm, cnt, sems.at[3]),
    ]
    for copy in copies:
        copy.start()
    skip = table[T_AGG + own0 + W] - AD
    resume = table[T_AGG + own2 + W] - AD
    writes = Writes([(0, skip), (resume, last + 1)], acc, coarse, out_sems)
    others = Writes([(last + 1, AD)], acc, coarse, out_sems)
    run = all_rows(
        ((count, own0), (own2, rows)), False, count, 0, 0, nbr, cnt, table, blocks, window, applied, turned, items, row_sems, a_hbm, acc, writes
    )
    clear(acc, HALF + 1, HALF + 1 + skip * KC)
    clear(acc, HALF + 1 + resume * KC, HALF + 1 + AD * KC)
    merge[T_N] = 0
    merge[T_H] = 0

    @pl.when(pos + 1 < devices)
    def _():
        begins = [table[T_NEXT + at] for at in range(4)]
        scan_rows(pos + 1, devices, rows, begins, merge)
        scan_sent(rows, begins, merge, True)

    split = merge[T_H]

    def add(slot, carry):
        acc[HALF + 1 + merge[T_DST + slot]] += got[slot - split].astype(jnp.float32)
        return carry

    lax.fori_loop(split, merge[T_N], add, 0)
    others.start(last + 1, AD)
    for at in range(W):
        window[W + rows + at] = got[HALF + at]
    copies[2].wait()
    copies[3].wait()
    copies[0].wait()
    copies[1].wait()
    run()
    for at in range(KC):
        edge[at] = acc[HALF + 1 + last * KC + at]
    merge[T_LAST] = last
    writes.wait()
    others.wait()


def merge_kernel(merge, got, edge, _, coarse, held, sems):
    last = merge[T_LAST] * KC

    def store(slot):
        return pltpu.make_async_copy(held.at[slot], coarse.at[merge[T_DST + slot]], sems.at[slot])

    def start(slot, carry):
        at = merge[T_DST + slot] - last
        base = edge[jnp.minimum(at, KC - 1)]
        held[slot] = got[slot].astype(jnp.float32) + jnp.where(at < KC, base, jnp.zeros_like(base))
        store(slot).start()
        return carry

    def wait(slot, carry):
        store(slot).wait()
        return carry

    lax.fori_loop(0, merge[T_H], start, 0)
    lax.fori_loop(0, merge[T_H], wait, 0)


SMEM = pl.BlockSpec(memory_space=pltpu.SMEM)
VMEM = pl.BlockSpec(memory_space=pltpu.VMEM)
HBM = pl.BlockSpec(memory_space=pltpu.HBM)
DMA = pltpu.SemaphoreType.DMA


def params(size=58):
    return pltpu.CompilerParams(vmem_limit_bytes=size * 1024 * 1024)


def cost(flops, moved):
    return pl.CostEstimate(flops=flops, bytes_accessed=moved, transcendentals=0)


def passed(block, step):
    devices = range(lax.axis_size(AXES))
    return lax.ppermute(block, AXES, [(i, i + step) for i in devices if i + step in devices])


def shards(a_blocks, nbr_offset, nbr_count, prolong, owner_start):
    devices = lax.axis_size(AXES)
    rows, slots, size, width = a_blocks.shape
    flops = rows * slots * size * size * width * 2
    moved = rows * slots * size * width * 2
    work = [
        pltpu.SMEM(nbr_offset.shape[::-1], jnp.int32),
        pltpu.SMEM(nbr_count.shape, jnp.int32),
        pltpu.VMEM((rows, slots, size, size), jnp.bfloat16),
        pltpu.VMEM((rows + 2 * W, size, width), jnp.bfloat16),
        [pltpu.VMEM((size, NQ * width), jnp.bfloat16)] * UNROLL,
        [pltpu.VMEM((width, size), jnp.bfloat16)] * UNROLL,
        pltpu.SMEM(((2 * W // NQ + 1) * (rows + 1),), jnp.int32),
        pltpu.VMEM((HALF + 1 + AD * KC, width, width), jnp.float32),
        DMA((4,)),
        DMA((rows,)),
        DMA((AD,)),
    ]
    table_shape = jax.ShapeDtypeStruct((T_LEN,), jnp.int32)
    coarse_shape = jax.ShapeDtypeStruct((AD * KC, width, width), jnp.float32)
    offsets = nbr_offset.T

    late, tail, coarse, table = pl.pallas_call(
        functools.partial(late_kernel, devices),
        out_shape=(
            jax.ShapeDtypeStruct((HALF + W, width, width), jnp.bfloat16),
            jax.ShapeDtypeStruct((W, size, width), jnp.bfloat16),
            coarse_shape,
            table_shape,
        ),
        in_specs=[HBM] * 5,
        out_specs=(VMEM, VMEM, HBM, SMEM),
        scratch_shapes=[pltpu.SMEM(owner_start.shape, jnp.int32)] + work,
        compiler_params=params(),
        cost_estimate=cost(flops // 3, moved // 3),
        name="late_rows",
    )(owner_start, offsets, nbr_count, a_blocks, prolong)
    before = passed(tail, 1)
    got_late = passed(late, -1)
    early, coarse = pl.pallas_call(
        functools.partial(early_kernel, devices),
        out_shape=(jax.ShapeDtypeStruct((HALF, width, width), jnp.bfloat16), coarse_shape),
        in_specs=[SMEM] + [HBM] * 6,
        out_specs=(VMEM, HBM),
        scratch_shapes=work,
        input_output_aliases={6: 1},
        compiler_params=params(50),
        cost_estimate=cost(flops // 3, moved // 3),
        name="early_rows",
    )(table, offsets, nbr_count, a_blocks, prolong, before, coarse)
    got_early = passed(early, -1)
    coarse, edge, merge = pl.pallas_call(
        functools.partial(own_kernel, devices),
        out_shape=(coarse_shape, jax.ShapeDtypeStruct((KC, width, width), jnp.float32), table_shape),
        in_specs=[SMEM] + [HBM] * 5 + [VMEM, HBM],
        out_specs=(HBM, VMEM, SMEM),
        scratch_shapes=work,
        input_output_aliases={7: 0},
        compiler_params=params(50),
        cost_estimate=cost(flops // 3, moved // 3),
        name="own_rows",
    )(table, offsets, nbr_count, a_blocks, prolong, before, got_late, coarse)
    coarse = pl.pallas_call(
        merge_kernel,
        out_shape=coarse_shape,
        in_specs=[SMEM, VMEM, VMEM, HBM],
        out_specs=HBM,
        scratch_shapes=[pltpu.VMEM((HALF, width, width), jnp.float32), DMA((HALF,))],
        input_output_aliases={3: 0},
        compiler_params=params(32),
        name="merge_rows",
    )(merge, got_early, edge, coarse)
    return coarse.reshape(AD, KC, width, width)


def solution(mesh):
    placed = (
        P(("dom", "sub"), None, None, None),
        P(("dom", "sub"), None),
        P(("dom", "sub")),
        P(("dom", "sub"), None, None),
        P(),
    )
    return jax.shard_map(
        shards,
        mesh=mesh,
        in_specs=placed,
        out_specs=P(("dom", "sub"), None, None, None),
        check_vma=False,
    )
```

```python
import functools

import jax
import jax.numpy as jnp
from jax import lax
from jax.experimental import pallas as pl
from jax.experimental.pallas import tpu as pltpu
from jax.sharding import PartitionSpec as P

W = 3
KC = 7
AD = 16
SMAX = 48
NQ = 2
UNROLL = 6
HALF = 25
EARLY = 18
AXES = ("dom", "sub")


AHEAD = 16
SHIFT = 20
FAR = 1024

T_AGG = 0
T_OFF = 128
T_BASE = 192
T_ROW = 256
T_DST = 384
T_CUM = 512
T_COLUMN = 640
T_N = 448
T_H = 449
T_LO = 450
T_HI = 451
T_S = 452
T_OWN0 = 453
T_OWN1 = 454
T_OWN2 = 455
T_LAST = 456
T_NEXT = 457
T_GROUP = 128
T_LEN = 768


def starts(pos, devices, rows, own_ref):
    def start(owner):
        at = jnp.clip(owner, 0, devices - 1)
        given = jnp.where(owner < devices, own_ref[at], devices * rows)
        return jnp.where(owner < 0, 0, given) - pos * rows

    return [start(pos + step) for step in (-1, 0, 1, 2)]


def row_start(begin, length, agg):
    return begin + lax.shift_right_logical(agg * length + (AD - 1), 4)


def scan_rows(pos, devices, rows, begins, table, upto):
    total = devices * rows
    first = pos * rows
    scale = []
    for owner in range(3):
        length = jnp.maximum(begins[owner + 1] - begins[owner], 1)
        scale.append(lax.div(length + (2**SHIFT - 1), length) * AD)
    items = jnp.int32(0)
    aggs = []
    for at in range(upto + 2 * W):
        row = at - W

        def local(owner):
            return lax.shift_right_logical((row - begins[owner]) * scale[owner], SHIFT) + owner * AD

        if row >= rows:
            agg = jnp.where(row >= begins[2], local(2), local(1))
            agg = jnp.where(first + row < total, agg, aggs[-1])
            column = jnp.where(first + row < total, agg, FAR)
        elif row >= SMAX:
            agg = column = local(1)
        elif row >= 0:
            agg = column = jnp.where(row >= begins[1], local(1), local(0))
        else:
            agg = jnp.where(first > 0, local(0), AD)
            column = jnp.where(first > 0, agg, FAR)
        aggs.append(agg)
        table[T_AGG + at] = agg
        if upto == rows:
            table[T_COLUMN + at] = column
        if at >= 2 * W:
            table[T_CUM + at - 2 * W] = items
            items = items + (lax.shift_right_logical(agg - aggs[at - 2 * W], 1) + 1)
    table[T_CUM + upto] = items


def scan_sent(begins, table, places):
    count = begins[1]
    length = begins[1] - begins[0]
    sent = table[T_CUM + count]
    share = lax.shift_right_logical(7 * sent, 4)
    lowest = jnp.where(count > 0, table[T_AGG + W], AD)

    def span(agg):
        return (
            jnp.maximum(row_start(begins[0], length, agg), 0),
            jnp.minimum(row_start(begins[0], length, agg + 1), count),
        )

    def step(agg, carry):
        end, floor, even = carry
        row, stop = span(agg)
        off = end - table[T_AGG + row]
        table[T_OFF + agg] = off
        table[T_BASE + agg] = end
        table[T_ROW + agg] = row
        begin = end
        end = off + table[T_AGG + stop - 1 + 2 * W] + 1
        if places:

            def put(slot, carry):
                table[T_DST + slot] = (KC - 1) * agg + W + slot - off
                return carry

            lax.fori_loop(begin, end, put, 0)
        floor = jnp.where(row < W, end, floor)
        even = jnp.where(sent - table[T_CUM + row] > share, end, even)
        return end, floor, even

    end, floor, even = lax.fori_loop(lowest, AD, step, (0, 0, 0))
    split = jnp.maximum(jnp.maximum(end - HALF, floor), jnp.minimum(even, EARLY))
    table[T_N] = end
    table[T_H] = split
    if places:
        return

    def find(agg, carry):
        low, high = carry
        base = table[T_BASE + agg]
        row, stop = span(agg)
        low = jnp.where(base <= split, row, low)
        high = jnp.where(base < split, stop, high)
        return low, high

    low, high = lax.fori_loop(lowest, AD, find, (0, 0))
    table[T_LO] = jnp.where(split >= end, count, low)
    table[T_HI] = high


def share_own(rows, begins, table):
    count = begins[1]
    length = begins[2] - begins[1]
    whole = table[T_CUM + rows]
    first = jnp.maximum(lax.div(whole, 3) - table[T_CUM + count] + table[T_CUM + table[T_LO]], 0)
    second = jnp.maximum(lax.div(3 * whole, 8) - table[T_CUM + table[T_HI]], 0)

    def step(agg, carry):
        own0, own1, own2 = carry
        row = row_start(count, length, agg)
        fresh = (row >= W) & (own0 < 0)
        own0 = jnp.where(fresh, row, own0)
        own1 = jnp.where(fresh, row, own1)
        own2 = jnp.where(fresh, row, own2)
        inside = (own0 >= 0) & (row <= rows - W)
        done = table[T_CUM + row]
        own1 = jnp.where(inside & (done <= table[T_CUM + jnp.maximum(own0, 0)] + first), row, own1)
        own2 = jnp.where(inside & (done <= table[T_CUM + jnp.maximum(own1, 0)] + second), row, own2)
        return own0, own1, own2

    own0, own1, own2 = lax.fori_loop(0, AD, step, (-1, -1, -1))
    table[T_OWN0] = own0
    table[T_OWN1] = own1
    table[T_OWN2] = own2
    table[T_S] = count
    table[T_LAST] = table[T_AGG + rows - 1 + W] - AD


def apply_row(row, group, nbr, cnt, table, blocks, window, applied):
    right = []
    left = []
    slots = cnt[row]
    lowest = table[T_AGG + row] + NQ * group
    for k in range(blocks.shape[1]):
        at = row + W + nbr[k, row]
        near = window[at]
        column = jnp.where(k < slots, table[T_COLUMN + at], FAR) - lowest
        zero = jnp.zeros_like(near)
        right.append(jnp.concatenate([jnp.where(column == q, near, zero) for q in range(NQ)], axis=1))
        left.append(blocks[row, k])
    applied[...] = jnp.dot(
        jnp.concatenate(left, axis=1), jnp.concatenate(right, axis=0), preferred_element_type=jnp.float32
    ).astype(applied.dtype)


def all_rows(ranges, down, ahead, low_slot, high_slot, nbr, cnt, table, blocks, window, applied, turned, items, row_sems, a_hbm, acc, writes):
    (lo0, hi0), (lo1, hi1) = ranges
    width = window.shape[2]
    count = table[T_S]
    turn = hi0 - lo0

    def row_at(index):
        sent = hi0 - 1 - index if down else lo0 + index
        return jnp.where(index < turn, sent, lo1 + index - turn)

    def start(index, amount):
        row = row_at(index)

        @pl.when((row < ahead) | (row >= count))
        def _():
            pltpu.make_async_copy(a_hbm.at[row], blocks.at[row], row_sems.at[row]).start()

        for group in range((2 * W) // NQ + 1):
            items[amount + group] = row + T_GROUP * group
        return amount + table[T_CUM + row + 1] - table[T_CUM + row]

    amount = lax.fori_loop(0, turn + hi1 - lo1, start, 0)

    def item(index):
        at = items[jnp.clip(index, 0, amount - 1)]
        valid = (index >= 0) & (index < amount)
        return at & (T_GROUP - 1), lax.shift_right_logical(at, 7), valid

    def add(row, group, valid, u):
        term = jnp.dot(turned[u][...], applied[u][...], preferred_element_type=jnp.float32)
        agg = table[T_AGG + row + W]
        highest = table[T_AGG + row + 2 * W]
        own = row >= count
        for q in range(NQ):
            target = table[T_AGG + row] + NQ * group + q
            sent = table[T_OFF + agg] + target
            kept = (KC - 1) * agg - KC * AD + W + target
            ok = valid & (target <= highest) & (own | ((sent >= low_slot) & (sent < high_slot)))
            at = jnp.where(ok, jnp.where(own, HALF + 1 + kept, sent - low_slot), HALF)
            acc[at] += term[:, q * width : (q + 1) * width]

    def add_block(begin):
        for u in range(UNROLL):
            row, group, valid = item(begin + u)
            add(row, group, valid, u)

    def block(step, written):
        begin = step * UNROLL
        row, _, valid = item(begin - UNROLL)
        whole = jnp.where(valid, jnp.clip(table[T_AGG + row + W] - AD, 0, AD), 0)
        writes.start(written, whole)
        for u in range(UNROLL):
            row, group, valid = item(begin + u)

            @pl.when(valid & (group == 0))
            def _():
                pltpu.make_async_copy(a_hbm.at[row], blocks.at[row], row_sems.at[row]).wait()

        add_block(begin - UNROLL)
        for u in range(UNROLL):
            row, group, valid = item(begin + u)
            apply_row(row, group, nbr, cnt, table, blocks, window, applied[u])
            turned[u][...] = window[row + W].T
        return jnp.maximum(written, whole)

    def run():
        @pl.when(amount > 0)
        def _():
            steps = lax.div(amount + UNROLL - 1, UNROLL)
            written = lax.fori_loop(0, steps, block, jnp.int32(0))
            add_block((steps - 1) * UNROLL)
            writes.start(written, AD)

    return run


def clear_own(acc, begin, end):
    def step(agg, carry):
        acc[pl.ds(HALF + 1 + agg * KC, KC)] = jnp.zeros((KC,) + acc.shape[1:], acc.dtype)
        return carry

    lax.fori_loop(begin, end, step, 0)


def give(acc, out, amount):
    def step(at, carry):
        out[at] = acc[at].astype(out.dtype)
        return carry

    lax.fori_loop(0, amount, step, 0)


class Writes:
    def __init__(self, ranges, acc, coarse, sems):
        self.ranges, self.acc, self.coarse, self.sems = ranges, acc, coarse, sems

    def each(self, begin, end, act):
        def step(agg, carry):
            inside = False
            for low, high in self.ranges:
                inside = inside | ((agg >= low) & (agg < high))

            @pl.when(inside)
            def _():
                act(
                    pltpu.make_async_copy(
                        self.acc.at[pl.ds(HALF + 1 + agg * KC, KC)],
                        self.coarse.at[pl.ds(agg * KC, KC)],
                        self.sems.at[agg],
                    )
                )

            return carry

        lax.fori_loop(begin, end, step, 0)

    def start(self, begin, end):
        self.each(begin, end, lambda copy: copy.start())

    def wait(self):
        self.each(0, AD, lambda copy: copy.wait())


def position():
    place = 0
    for axis in AXES:
        place = place * lax.axis_size(axis) + lax.axis_index(axis)
    return place


def late_kernel(
    devices, own_hbm, nbr_hbm, cnt_hbm, a_hbm, p_hbm, out, tail, coarse, table, own, nbr, cnt, blocks, window, applied, turned, items, acc, sems, row_sems, out_sems
):
    rows = a_hbm.shape[0]
    pos = position()
    copies = [
        pltpu.make_async_copy(own_hbm, own, sems.at[0]),
        pltpu.make_async_copy(nbr_hbm, nbr, sems.at[1]),
        pltpu.make_async_copy(cnt_hbm, cnt, sems.at[2]),
        pltpu.make_async_copy(p_hbm, window.at[pl.ds(W, rows)], sems.at[3]),
    ]
    for copy in copies:
        copy.start()
    copies[0].wait()
    begins = starts(pos, devices, rows, own)
    for at, begin in enumerate(starts(pos + 1, devices, rows, own)):
        table[T_NEXT + at] = begin
    count = begins[1]
    ahead = jnp.maximum(count - AHEAD, W)

    def fetch(row):
        return pltpu.make_async_copy(a_hbm.at[row], blocks.at[row], row_sems.at[row])

    def prefetch(index, carry):
        fetch(count - 1 - index).start()
        return carry

    def drain(row, carry):
        fetch(row).wait()
        return carry

    lax.fori_loop(0, count - ahead, prefetch, 0)
    scan_rows(pos, devices, rows, begins, table, rows)
    scan_sent(begins, table, False)
    share_own(rows, begins, table)
    low, own0, own1 = table[T_LO], table[T_OWN0], table[T_OWN1]
    begin = table[T_AGG + own0 + W] - AD
    stop = table[T_AGG + own1 + W] - AD
    writes = Writes([(begin, stop)], acc, coarse, out_sems)
    run = all_rows(
        ((low, count), (own0, own1)), True, ahead, table[T_H], table[T_N], nbr, cnt, table, blocks, window, applied, turned, items, row_sems, a_hbm, acc, writes
    )
    acc[0:HALF] = jnp.zeros((HALF,) + acc.shape[1:], acc.dtype)
    clear_own(acc, begin, stop)
    copies[1].wait()
    copies[2].wait()
    copies[3].wait()
    for at in range(W):
        out[HALF + at] = window[W + at]
        tail[at] = window[rows + at]
    run()
    give(acc, out, HALF)
    lax.fori_loop(ahead, low, drain, 0)
    writes.wait()


def early_kernel(
    devices, table, nbr_hbm, cnt_hbm, a_hbm, p_hbm, before, _, out, coarse, nbr, cnt, blocks, window, applied, turned, items, acc, sems, row_sems, out_sems
):
    rows = a_hbm.shape[0]
    pos = position()
    own1, own2 = table[T_OWN1], table[T_OWN2]
    copies = [
        pltpu.make_async_copy(p_hbm, window.at[pl.ds(W, rows)], sems.at[0]),
        pltpu.make_async_copy(before, window.at[pl.ds(0, W)], sems.at[1]),
        pltpu.make_async_copy(nbr_hbm, nbr, sems.at[2]),
        pltpu.make_async_copy(cnt_hbm, cnt, sems.at[3]),
    ]
    for copy in copies:
        copy.start()
    begin = table[T_AGG + own1 + W] - AD
    stop = table[T_AGG + own2 + W] - AD
    writes = Writes([(begin, stop)], acc, coarse, out_sems)
    run = all_rows(
        ((0, table[T_HI]), (own1, own2)), False, table[T_S], 0, table[T_H], nbr, cnt, table, blocks, window, applied, turned, items, row_sems, a_hbm, acc, writes
    )
    acc[0:HALF] = jnp.zeros((HALF,) + acc.shape[1:], acc.dtype)
    clear_own(acc, begin, stop)
    copies[2].wait()
    copies[3].wait()
    copies[0].wait()
    copies[1].wait()
    run()
    give(acc, out, EARLY)
    writes.wait()


def own_kernel(
    devices, table, nbr_hbm, cnt_hbm, a_hbm, p_hbm, before, got, _, coarse, edge, merge, nbr, cnt, blocks, window, applied, turned, items, acc, sems, row_sems, out_sems
):
    rows = a_hbm.shape[0]
    pos = position()
    count, own0, own2, last = table[T_S], table[T_OWN0], table[T_OWN2], table[T_LAST]
    copies = [
        pltpu.make_async_copy(p_hbm, window.at[pl.ds(W, rows)], sems.at[0]),
        pltpu.make_async_copy(before, window.at[pl.ds(0, W)], sems.at[1]),
        pltpu.make_async_copy(nbr_hbm, nbr, sems.at[2]),
        pltpu.make_async_copy(cnt_hbm, cnt, sems.at[3]),
    ]
    for copy in copies:
        copy.start()
    skip = table[T_AGG + own0 + W] - AD
    resume = table[T_AGG + own2 + W] - AD
    writes = Writes([(0, skip), (resume, last + 1)], acc, coarse, out_sems)
    others = Writes([(last + 1, AD)], acc, coarse, out_sems)
    run = all_rows(
        ((count, own0), (own2, rows)), False, count, 0, 0, nbr, cnt, table, blocks, window, applied, turned, items, row_sems, a_hbm, acc, writes
    )
    clear_own(acc, 0, skip)
    clear_own(acc, resume, AD)
    merge[T_N] = 0
    merge[T_H] = 0

    @pl.when(pos + 1 < devices)
    def _():
        begins = [table[T_NEXT + at] for at in range(4)]
        scan_rows(pos + 1, devices, rows, begins, merge, SMAX)
        scan_sent(begins, merge, True)

    split = merge[T_H]

    def add(slot, carry):
        acc[HALF + 1 + merge[T_DST + slot]] += got[slot - split].astype(jnp.float32)
        return carry

    lax.fori_loop(split, merge[T_N], add, 0)
    others.start(last + 1, AD)
    for at in range(W):
        window[W + rows + at] = got[HALF + at]
    copies[2].wait()
    copies[3].wait()
    copies[0].wait()
    copies[1].wait()
    run()
    for at in range(KC):
        edge[at] = acc[HALF + 1 + last * KC + at]
    merge[T_LAST] = last
    writes.wait()
    others.wait()


def merge_kernel(merge, got, edge, _, coarse, held, sems):
    last = merge[T_LAST] * KC

    def store(slot):
        return pltpu.make_async_copy(held.at[slot], coarse.at[merge[T_DST + slot]], sems.at[slot])

    def start(slot, carry):
        at = merge[T_DST + slot] - last
        base = edge[jnp.minimum(at, KC - 1)]
        held[slot] = got[slot].astype(jnp.float32) + jnp.where(at < KC, base, jnp.zeros_like(base))
        store(slot).start()
        return carry

    def wait(slot, carry):
        store(slot).wait()
        return carry

    lax.fori_loop(0, merge[T_H], start, 0)
    lax.fori_loop(0, merge[T_H], wait, 0)


SMEM = pl.BlockSpec(memory_space=pltpu.SMEM)
VMEM = pl.BlockSpec(memory_space=pltpu.VMEM)
HBM = pl.BlockSpec(memory_space=pltpu.HBM)
DMA = pltpu.SemaphoreType.DMA


def params(size=58):
    return pltpu.CompilerParams(vmem_limit_bytes=size * 1024 * 1024)


def cost(flops, moved):
    return pl.CostEstimate(flops=flops, bytes_accessed=moved, transcendentals=0)


def passed(block, step):
    devices = range(lax.axis_size(AXES))
    return lax.ppermute(block, AXES, [(i, i + step) for i in devices if i + step in devices])


def shards(a_blocks, nbr_offset, nbr_count, prolong, owner_start):
    devices = lax.axis_size(AXES)
    rows, slots, size, width = a_blocks.shape
    flops = rows * slots * size * size * width * 2
    moved = rows * slots * size * width * 2
    work = [
        pltpu.SMEM(nbr_offset.shape[::-1], jnp.int32),
        pltpu.SMEM(nbr_count.shape, jnp.int32),
        pltpu.VMEM((rows, slots, size, size), jnp.bfloat16),
        pltpu.VMEM((rows + 2 * W, size, width), jnp.bfloat16),
        [pltpu.VMEM((size, NQ * width), jnp.bfloat16)] * UNROLL,
        [pltpu.VMEM((width, size), jnp.bfloat16)] * UNROLL,
        pltpu.SMEM(((2 * W // NQ + 1) * (rows + 1),), jnp.int32),
        pltpu.VMEM((HALF + 1 + AD * KC, width, width), jnp.float32),
        DMA((4,)),
        DMA((rows,)),
        DMA((AD,)),
    ]
    table_shape = jax.ShapeDtypeStruct((T_LEN,), jnp.int32)
    coarse_shape = jax.ShapeDtypeStruct((AD * KC, width, width), jnp.float32)
    offsets = nbr_offset.T

    late, tail, coarse, table = pl.pallas_call(
        functools.partial(late_kernel, devices),
        out_shape=(
            jax.ShapeDtypeStruct((HALF + W, width, width), jnp.bfloat16),
            jax.ShapeDtypeStruct((W, size, width), jnp.bfloat16),
            coarse_shape,
            table_shape,
        ),
        in_specs=[HBM] * 5,
        out_specs=(VMEM, VMEM, HBM, SMEM),
        scratch_shapes=[pltpu.SMEM(owner_start.shape, jnp.int32)] + work,
        compiler_params=params(),
        cost_estimate=cost(flops // 3, moved // 3),
        name="late_rows",
    )(owner_start, offsets, nbr_count, a_blocks, prolong)
    before = passed(tail, 1)
    got_late = passed(late, -1)
    early, coarse = pl.pallas_call(
        functools.partial(early_kernel, devices),
        out_shape=(jax.ShapeDtypeStruct((EARLY, width, width), jnp.bfloat16), coarse_shape),
        in_specs=[SMEM] + [HBM] * 6,
        out_specs=(VMEM, HBM),
        scratch_shapes=work,
        input_output_aliases={6: 1},
        compiler_params=params(50),
        cost_estimate=cost(flops // 3, moved // 3),
        name="early_rows",
    )(table, offsets, nbr_count, a_blocks, prolong, before, coarse)
    got_early = passed(early, -1)
    coarse, edge, merge = pl.pallas_call(
        functools.partial(own_kernel, devices),
        out_shape=(coarse_shape, jax.ShapeDtypeStruct((KC, width, width), jnp.float32), table_shape),
        in_specs=[SMEM] + [HBM] * 5 + [VMEM, HBM],
        out_specs=(HBM, VMEM, SMEM),
        scratch_shapes=work,
        input_output_aliases={7: 0},
        compiler_params=params(50),
        cost_estimate=cost(flops // 3, moved // 3),
        name="own_rows",
    )(table, offsets, nbr_count, a_blocks, prolong, before, got_late, coarse)
    coarse = pl.pallas_call(
        merge_kernel,
        out_shape=coarse_shape,
        in_specs=[SMEM, VMEM, VMEM, HBM],
        out_specs=HBM,
        scratch_shapes=[pltpu.VMEM((EARLY, width, width), jnp.float32), DMA((EARLY,))],
        input_output_aliases={3: 0},
        compiler_params=params(32),
        name="merge_rows",
    )(merge, got_early, edge, coarse)
    return coarse.reshape(AD, KC, width, width)


def solution(mesh):
    placed = (
        P(("dom", "sub"), None, None, None),
        P(("dom", "sub"), None),
        P(("dom", "sub")),
        P(("dom", "sub"), None, None),
        P(),
    )
    return jax.shard_map(
        shards,
        mesh=mesh,
        in_specs=placed,
        out_specs=P(("dom", "sub"), None, None, None),
        check_vma=False,
    )
```

```python
import functools

import jax
import jax.numpy as jnp
from jax import lax
from jax.experimental import pallas as pl
from jax.experimental.pallas import tpu as pltpu
from jax.sharding import PartitionSpec as P

W = 3
KC = 7
AD = 16
SMAX = 48
NQ = 2
UNROLL = 6
HALF = 22
EARLY = 21
AXES = ("dom", "sub")


AHEAD = 16
SHIFT = 20
FAR = 1024

T_AGG = 0
T_OFF = 128
T_BASE = 192
T_ROW = 256
T_DST = 384
T_CUM = 512
T_COLUMN = 640
T_N = 448
T_H = 449
T_LO = 450
T_HI = 451
T_S = 452
T_OWN0 = 453
T_OWN1 = 454
T_OWN2 = 455
T_LAST = 456
T_NEXT = 457
T_GROUP = 128
T_LEN = 768


def starts(pos, devices, rows, own_ref):
    def start(owner):
        at = jnp.clip(owner, 0, devices - 1)
        given = jnp.where(owner < devices, own_ref[at], devices * rows)
        return jnp.where(owner < 0, 0, given) - pos * rows

    return [start(pos + step) for step in (-1, 0, 1, 2)]


def row_start(begin, length, agg):
    return begin + lax.shift_right_logical(agg * length + (AD - 1), 4)


def scan_rows(pos, devices, rows, begins, table, upto):
    total = devices * rows
    first = pos * rows
    scale = []
    for owner in range(3):
        length = jnp.maximum(begins[owner + 1] - begins[owner], 1)
        scale.append(lax.div(length + (2**SHIFT - 1), length) * AD)
    items = jnp.int32(0)
    aggs = []
    for at in range(upto + 2 * W):
        row = at - W

        def local(owner):
            return lax.shift_right_logical((row - begins[owner]) * scale[owner], SHIFT) + owner * AD

        if row >= rows:
            agg = jnp.where(row >= begins[2], local(2), local(1))
            agg = jnp.where(first + row < total, agg, aggs[-1])
            column = jnp.where(first + row < total, agg, FAR)
        elif row >= SMAX:
            agg = column = local(1)
        elif row >= 0:
            agg = column = jnp.where(row >= begins[1], local(1), local(0))
        else:
            agg = jnp.where(first > 0, local(0), AD)
            column = jnp.where(first > 0, agg, FAR)
        aggs.append(agg)
        table[T_AGG + at] = agg
        if upto == rows:
            table[T_COLUMN + at] = column
        if at >= 2 * W:
            table[T_CUM + at - 2 * W] = items
            items = items + (lax.shift_right_logical(agg - aggs[at - 2 * W], 1) + 1)
    table[T_CUM + upto] = items


def scan_sent(begins, table, places):
    count = begins[1]
    length = begins[1] - begins[0]
    sent = table[T_CUM + count]
    share = lax.shift_right_logical(7 * sent, 4)
    lowest = jnp.where(count > 0, table[T_AGG + W], AD)

    def span(agg):
        return (
            jnp.maximum(row_start(begins[0], length, agg), 0),
            jnp.minimum(row_start(begins[0], length, agg + 1), count),
        )

    def step(agg, carry):
        end, floor, even = carry
        row, stop = span(agg)
        off = end - table[T_AGG + row]
        table[T_OFF + agg] = off
        table[T_BASE + agg] = end
        table[T_ROW + agg] = row
        begin = end
        end = off + table[T_AGG + stop - 1 + 2 * W] + 1
        if places:

            def put(slot, carry):
                table[T_DST + slot] = (KC - 1) * agg + W + slot - off
                return carry

            lax.fori_loop(begin, end, put, 0)
        floor = jnp.where(row < W, end, floor)
        even = jnp.where(sent - table[T_CUM + row] > share, end, even)
        return end, floor, even

    end, floor, even = lax.fori_loop(lowest, AD, step, (0, 0, 0))
    split = jnp.maximum(jnp.maximum(end - HALF, floor), jnp.minimum(even, EARLY))
    table[T_N] = end
    table[T_H] = split
    if places:
        return

    def find(agg, carry):
        low, high = carry
        base = table[T_BASE + agg]
        row, stop = span(agg)
        low = jnp.where(base <= split, row, low)
        high = jnp.where(base < split, stop, high)
        return low, high

    low, high = lax.fori_loop(lowest, AD, find, (0, 0))
    table[T_LO] = jnp.where(split >= end, count, low)
    table[T_HI] = high


def share_own(rows, begins, table):
    count = begins[1]
    length = begins[2] - begins[1]
    whole = table[T_CUM + rows]
    first = jnp.maximum(lax.div(whole, 3) - table[T_CUM + count] + table[T_CUM + table[T_LO]], 0)
    second = jnp.maximum(lax.div(3 * whole, 8) - table[T_CUM + table[T_HI]], 0)

    def step(agg, carry):
        own0, own1, own2 = carry
        row = row_start(count, length, agg)
        fresh = (row >= W) & (own0 < 0)
        own0 = jnp.where(fresh, row, own0)
        own1 = jnp.where(fresh, row, own1)
        own2 = jnp.where(fresh, row, own2)
        inside = (own0 >= 0) & (row <= rows - W)
        done = table[T_CUM + row]
        own1 = jnp.where(inside & (done <= table[T_CUM + jnp.maximum(own0, 0)] + first), row, own1)
        own2 = jnp.where(inside & (done <= table[T_CUM + jnp.maximum(own1, 0)] + second), row, own2)
        return own0, own1, own2

    own0, own1, own2 = lax.fori_loop(0, AD, step, (-1, -1, -1))
    table[T_OWN0] = own0
    table[T_OWN1] = own1
    table[T_OWN2] = own2
    table[T_S] = count
    table[T_LAST] = table[T_AGG + rows - 1 + W] - AD


def apply_row(row, group, nbr, cnt, table, blocks, window, applied):
    right = []
    left = []
    slots = cnt[row]
    lowest = table[T_AGG + row] + NQ * group
    for k in range(blocks.shape[1]):
        at = row + W + nbr[k, row]
        near = window[at]
        column = jnp.where(k < slots, table[T_COLUMN + at], FAR) - lowest
        zero = jnp.zeros_like(near)
        right.append(jnp.concatenate([jnp.where(column == q, near, zero) for q in range(NQ)], axis=1))
        left.append(blocks[row, k])
    applied[...] = jnp.dot(
        jnp.concatenate(left, axis=1), jnp.concatenate(right, axis=0), preferred_element_type=jnp.float32
    ).astype(applied.dtype)


def all_rows(ranges, down, ahead, low_slot, high_slot, nbr, cnt, table, blocks, window, applied, turned, items, row_sems, a_hbm, acc, writes):
    (lo0, hi0), (lo1, hi1) = ranges
    width = window.shape[2]
    count = table[T_S]
    turn = hi0 - lo0

    def row_at(index):
        sent = hi0 - 1 - index if down else lo0 + index
        return jnp.where(index < turn, sent, lo1 + index - turn)

    def start(index, amount):
        row = row_at(index)

        @pl.when((row < ahead) | (row >= count))
        def _():
            pltpu.make_async_copy(a_hbm.at[row], blocks.at[row], row_sems.at[row]).start()

        for group in range((2 * W) // NQ + 1):
            items[amount + group] = row + T_GROUP * group
        return amount + table[T_CUM + row + 1] - table[T_CUM + row]

    amount = lax.fori_loop(0, turn + hi1 - lo1, start, 0)

    def item(index):
        at = items[jnp.clip(index, 0, amount - 1)]
        valid = (index >= 0) & (index < amount)
        return at & (T_GROUP - 1), lax.shift_right_logical(at, 7), valid

    def add(row, group, valid, u):
        term = jnp.dot(turned[u][...], applied[u][...], preferred_element_type=jnp.float32)
        agg = table[T_AGG + row + W]
        highest = table[T_AGG + row + 2 * W]
        own = row >= count
        for q in range(NQ):
            target = table[T_AGG + row] + NQ * group + q
            sent = table[T_OFF + agg] + target
            kept = (KC - 1) * agg - KC * AD + W + target
            ok = valid & (target <= highest) & (own | ((sent >= low_slot) & (sent < high_slot)))
            at = jnp.where(ok, jnp.where(own, HALF + 1 + kept, sent - low_slot), HALF)
            acc[at] += term[:, q * width : (q + 1) * width]

    def add_block(begin):
        for u in range(UNROLL):
            row, group, valid = item(begin + u)
            add(row, group, valid, u)

    def block(step, written):
        begin = step * UNROLL
        row, _, valid = item(begin - UNROLL)
        whole = jnp.where(valid, jnp.clip(table[T_AGG + row + W] - AD, 0, AD), 0)
        writes.start(written, whole)
        for u in range(UNROLL):
            row, group, valid = item(begin + u)

            @pl.when(valid & (group == 0))
            def _():
                pltpu.make_async_copy(a_hbm.at[row], blocks.at[row], row_sems.at[row]).wait()

        add_block(begin - UNROLL)
        for u in range(UNROLL):
            row, group, valid = item(begin + u)
            apply_row(row, group, nbr, cnt, table, blocks, window, applied[u])
            turned[u][...] = window[row + W].T
        return jnp.maximum(written, whole)

    def run():
        @pl.when(amount > 0)
        def _():
            steps = lax.div(amount + UNROLL - 1, UNROLL)
            written = lax.fori_loop(0, steps, block, jnp.int32(0))
            add_block((steps - 1) * UNROLL)
            writes.start(written, AD)

    return run


def clear_own(acc, begin, end):
    def step(agg, carry):
        acc[pl.ds(HALF + 1 + agg * KC, KC)] = jnp.zeros((KC,) + acc.shape[1:], acc.dtype)
        return carry

    lax.fori_loop(begin, end, step, 0)


def give(acc, out, amount):
    def step(at, carry):
        out[at] = acc[at].astype(out.dtype)
        return carry

    lax.fori_loop(0, amount, step, 0)


class Writes:
    def __init__(self, ranges, acc, coarse, sems):
        self.ranges, self.acc, self.coarse, self.sems = ranges, acc, coarse, sems

    def each(self, begin, end, act):
        def step(agg, carry):
            inside = False
            for low, high in self.ranges:
                inside = inside | ((agg >= low) & (agg < high))

            @pl.when(inside)
            def _():
                act(
                    pltpu.make_async_copy(
                        self.acc.at[pl.ds(HALF + 1 + agg * KC, KC)],
                        self.coarse.at[pl.ds(agg * KC, KC)],
                        self.sems.at[agg],
                    )
                )

            return carry

        lax.fori_loop(begin, end, step, 0)

    def start(self, begin, end):
        self.each(begin, end, lambda copy: copy.start())

    def wait(self):
        self.each(0, AD, lambda copy: copy.wait())


def position():
    place = 0
    for axis in AXES:
        place = place * lax.axis_size(axis) + lax.axis_index(axis)
    return place


def late_kernel(
    devices, own_hbm, nbr_hbm, cnt_hbm, a_hbm, p_hbm, out, tail, coarse, table, own, nbr, cnt, blocks, window, applied, turned, items, acc, sems, row_sems, out_sems
):
    rows = a_hbm.shape[0]
    pos = position()
    copies = [
        pltpu.make_async_copy(own_hbm, own, sems.at[0]),
        pltpu.make_async_copy(nbr_hbm, nbr, sems.at[1]),
        pltpu.make_async_copy(cnt_hbm, cnt, sems.at[2]),
        pltpu.make_async_copy(p_hbm, window.at[pl.ds(W, rows)], sems.at[3]),
    ]
    for copy in copies:
        copy.start()
    copies[0].wait()
    begins = starts(pos, devices, rows, own)
    for at, begin in enumerate(starts(pos + 1, devices, rows, own)):
        table[T_NEXT + at] = begin
    count = begins[1]
    ahead = jnp.maximum(count - AHEAD, W)

    def fetch(row):
        return pltpu.make_async_copy(a_hbm.at[row], blocks.at[row], row_sems.at[row])

    def prefetch(index, carry):
        fetch(count - 1 - index).start()
        return carry

    def drain(row, carry):
        fetch(row).wait()
        return carry

    lax.fori_loop(0, count - ahead, prefetch, 0)
    scan_rows(pos, devices, rows, begins, table, rows)
    scan_sent(begins, table, False)
    share_own(rows, begins, table)
    low, own0, own1 = table[T_LO], table[T_OWN0], table[T_OWN1]
    begin = table[T_AGG + own0 + W] - AD
    stop = table[T_AGG + own1 + W] - AD
    writes = Writes([(begin, stop)], acc, coarse, out_sems)
    run = all_rows(
        ((low, count), (own0, own1)), True, ahead, table[T_H], table[T_N], nbr, cnt, table, blocks, window, applied, turned, items, row_sems, a_hbm, acc, writes
    )
    acc[0:HALF] = jnp.zeros((HALF,) + acc.shape[1:], acc.dtype)
    clear_own(acc, begin, stop)
    copies[1].wait()
    copies[2].wait()
    copies[3].wait()
    for at in range(W):
        out[HALF + at] = window[W + at]
        tail[at] = window[rows + at]
    run()
    give(acc, out, HALF)
    lax.fori_loop(ahead, low, drain, 0)
    writes.wait()


def early_kernel(
    devices, table, nbr_hbm, cnt_hbm, a_hbm, p_hbm, before, _, out, coarse, nbr, cnt, blocks, window, applied, turned, items, acc, sems, row_sems, out_sems
):
    rows = a_hbm.shape[0]
    pos = position()
    own1, own2 = table[T_OWN1], table[T_OWN2]
    copies = [
        pltpu.make_async_copy(p_hbm, window.at[pl.ds(W, rows)], sems.at[0]),
        pltpu.make_async_copy(before, window.at[pl.ds(0, W)], sems.at[1]),
        pltpu.make_async_copy(nbr_hbm, nbr, sems.at[2]),
        pltpu.make_async_copy(cnt_hbm, cnt, sems.at[3]),
    ]
    for copy in copies:
        copy.start()
    begin = table[T_AGG + own1 + W] - AD
    stop = table[T_AGG + own2 + W] - AD
    writes = Writes([(begin, stop)], acc, coarse, out_sems)
    run = all_rows(
        ((0, table[T_HI]), (own1, own2)), False, table[T_S], 0, table[T_H], nbr, cnt, table, blocks, window, applied, turned, items, row_sems, a_hbm, acc, writes
    )
    acc[0:HALF] = jnp.zeros((HALF,) + acc.shape[1:], acc.dtype)
    clear_own(acc, begin, stop)
    copies[2].wait()
    copies[3].wait()
    copies[0].wait()
    copies[1].wait()
    run()
    give(acc, out, EARLY)
    writes.wait()


def own_kernel(
    devices, table, nbr_hbm, cnt_hbm, a_hbm, p_hbm, before, got, _, coarse, edge, merge, nbr, cnt, blocks, window, applied, turned, items, acc, sems, row_sems, out_sems
):
    rows = a_hbm.shape[0]
    pos = position()
    count, own0, own2, last = table[T_S], table[T_OWN0], table[T_OWN2], table[T_LAST]
    copies = [
        pltpu.make_async_copy(p_hbm, window.at[pl.ds(W, rows)], sems.at[0]),
        pltpu.make_async_copy(before, window.at[pl.ds(0, W)], sems.at[1]),
        pltpu.make_async_copy(nbr_hbm, nbr, sems.at[2]),
        pltpu.make_async_copy(cnt_hbm, cnt, sems.at[3]),
    ]
    for copy in copies:
        copy.start()
    skip = table[T_AGG + own0 + W] - AD
    resume = table[T_AGG + own2 + W] - AD
    writes = Writes([(0, skip), (resume, last + 1)], acc, coarse, out_sems)
    others = Writes([(last + 1, AD)], acc, coarse, out_sems)
    run = all_rows(
        ((count, own0), (own2, rows)), False, count, 0, 0, nbr, cnt, table, blocks, window, applied, turned, items, row_sems, a_hbm, acc, writes
    )
    clear_own(acc, 0, skip)
    clear_own(acc, resume, AD)
    merge[T_N] = 0
    merge[T_H] = 0

    @pl.when(pos + 1 < devices)
    def _():
        begins = [table[T_NEXT + at] for at in range(4)]
        scan_rows(pos + 1, devices, rows, begins, merge, SMAX)
        scan_sent(begins, merge, True)

    split = merge[T_H]

    def add(slot, carry):
        acc[HALF + 1 + merge[T_DST + slot]] += got[slot - split].astype(jnp.float32)
        return carry

    lax.fori_loop(split, merge[T_N], add, 0)
    others.start(last + 1, AD)
    for at in range(W):
        window[W + rows + at] = got[HALF + at]
    copies[2].wait()
    copies[3].wait()
    copies[0].wait()
    copies[1].wait()
    run()
    for at in range(KC):
        edge[at] = acc[HALF + 1 + last * KC + at]
    merge[T_LAST] = last
    writes.wait()
    others.wait()


def merge_kernel(merge, got, edge, _, coarse, held, sems):
    last = merge[T_LAST] * KC

    def store(slot):
        return pltpu.make_async_copy(held.at[slot], coarse.at[merge[T_DST + slot]], sems.at[slot])

    def start(slot, carry):
        at = merge[T_DST + slot] - last
        base = edge[jnp.minimum(at, KC - 1)]
        held[slot] = got[slot].astype(jnp.float32) + jnp.where(at < KC, base, jnp.zeros_like(base))
        store(slot).start()
        return carry

    def wait(slot, carry):
        store(slot).wait()
        return carry

    lax.fori_loop(0, merge[T_H], start, 0)
    lax.fori_loop(0, merge[T_H], wait, 0)


SMEM = pl.BlockSpec(memory_space=pltpu.SMEM)
VMEM = pl.BlockSpec(memory_space=pltpu.VMEM)
HBM = pl.BlockSpec(memory_space=pltpu.HBM)
DMA = pltpu.SemaphoreType.DMA


def params(size=58):
    return pltpu.CompilerParams(vmem_limit_bytes=size * 1024 * 1024)


def cost(flops, moved):
    return pl.CostEstimate(flops=flops, bytes_accessed=moved, transcendentals=0)


def passed(block, step):
    devices = range(lax.axis_size(AXES))
    return lax.ppermute(block, AXES, [(i, i + step) for i in devices if i + step in devices])


def shards(a_blocks, nbr_offset, nbr_count, prolong, owner_start):
    devices = lax.axis_size(AXES)
    rows, slots, size, width = a_blocks.shape
    flops = rows * slots * size * size * width * 2
    moved = rows * slots * size * width * 2
    work = [
        pltpu.SMEM(nbr_offset.shape[::-1], jnp.int32),
        pltpu.SMEM(nbr_count.shape, jnp.int32),
        pltpu.VMEM((rows, slots, size, size), jnp.bfloat16),
        pltpu.VMEM((rows + 2 * W, size, width), jnp.bfloat16),
        [pltpu.VMEM((size, NQ * width), jnp.bfloat16)] * UNROLL,
        [pltpu.VMEM((width, size), jnp.bfloat16)] * UNROLL,
        pltpu.SMEM(((2 * W // NQ + 1) * (rows + 1),), jnp.int32),
        pltpu.VMEM((HALF + 1 + AD * KC, width, width), jnp.float32),
        DMA((4,)),
        DMA((rows,)),
        DMA((AD,)),
    ]
    table_shape = jax.ShapeDtypeStruct((T_LEN,), jnp.int32)
    coarse_shape = jax.ShapeDtypeStruct((AD * KC, width, width), jnp.float32)
    offsets = nbr_offset.T

    late, tail, coarse, table = pl.pallas_call(
        functools.partial(late_kernel, devices),
        out_shape=(
            jax.ShapeDtypeStruct((HALF + W, width, width), jnp.bfloat16),
            jax.ShapeDtypeStruct((W, size, width), jnp.bfloat16),
            coarse_shape,
            table_shape,
        ),
        in_specs=[HBM] * 5,
        out_specs=(VMEM, VMEM, HBM, SMEM),
        scratch_shapes=[pltpu.SMEM(owner_start.shape, jnp.int32)] + work,
        compiler_params=params(),
        cost_estimate=cost(flops // 3, moved // 3),
        name="late_rows",
    )(owner_start, offsets, nbr_count, a_blocks, prolong)
    before = passed(tail, 1)
    got_late = passed(late, -1)
    early, coarse = pl.pallas_call(
        functools.partial(early_kernel, devices),
        out_shape=(jax.ShapeDtypeStruct((EARLY, width, width), jnp.bfloat16), coarse_shape),
        in_specs=[SMEM] + [HBM] * 6,
        out_specs=(VMEM, HBM),
        scratch_shapes=work,
        input_output_aliases={6: 1},
        compiler_params=params(50),
        cost_estimate=cost(flops // 3, moved // 3),
        name="early_rows",
    )(table, offsets, nbr_count, a_blocks, prolong, before, coarse)
    got_early = passed(early, -1)
    coarse, edge, merge = pl.pallas_call(
        functools.partial(own_kernel, devices),
        out_shape=(coarse_shape, jax.ShapeDtypeStruct((KC, width, width), jnp.float32), table_shape),
        in_specs=[SMEM] + [HBM] * 5 + [VMEM, HBM],
        out_specs=(HBM, VMEM, SMEM),
        scratch_shapes=work,
        input_output_aliases={7: 0},
        compiler_params=params(50),
        cost_estimate=cost(flops // 3, moved // 3),
        name="own_rows",
    )(table, offsets, nbr_count, a_blocks, prolong, before, got_late, coarse)
    coarse = pl.pallas_call(
        merge_kernel,
        out_shape=coarse_shape,
        in_specs=[SMEM, VMEM, VMEM, HBM],
        out_specs=HBM,
        scratch_shapes=[pltpu.VMEM((EARLY, width, width), jnp.float32), DMA((EARLY,))],
        input_output_aliases={3: 0},
        compiler_params=params(32),
        name="merge_rows",
    )(merge, got_early, edge, coarse)
    return coarse.reshape(AD, KC, width, width)


def solution(mesh):
    placed = (
        P(("dom", "sub"), None, None, None),
        P(("dom", "sub"), None),
        P(("dom", "sub")),
        P(("dom", "sub"), None, None),
        P(),
    )
    return jax.shard_map(
        shards,
        mesh=mesh,
        in_specs=placed,
        out_specs=P(("dom", "sub"), None, None, None),
        check_vma=False,
    )
```
